32 devices in a mesh: rows: 16 (over z, y, x), rep: 2 (over core).
Axes of the slice: x: 2, y: 2, z: 4, core: 2. Of those that a mesh axis runs over, the one named last changes fastest.
Arguments:
- features: bfloat16 [4096, 128], P('rows'), may hold values from -6 to 6
- weight: bfloat16 [128, 256], replicated, may hold values from -0.5 to 0.5
- bias: float32 [256], replicated, may hold values from -3 to 3
- block_count: int32 [2, 64], P('rep', 'rows'), may hold values from 1 to 16, as said below
- block_cols: int32 [2, 64, 16], P('rep', 'rows'), may hold values from 0 to 31, as said below
- block_vals: bfloat16 [2, 64, 16, 4096], P('rep', 'rows'), may hold values from -0.375 to 0.375
- cotangent: bfloat16 [4096, 256], P(('rows', 'rep')), may hold values from -0.1875 to 0.1875
Outputs:
- activated: bfloat16 [4096, 256], P(('rows', 'rep'))
- weight_grad: float32 [128, 256], P(None, 'rows')
- bias_grad: float32 [256], P('rows')
The draws below stay inside these ranges and needn't reach their ends.
Inputs may be any that keep to these rules, and one draw needn't show every extreme that they name: `block_count`: every draw has a block row with exactly 16 blocks in each half; counts are skewed by node range. `block_cols`: the column blocks of one block row and half are all different; slots at or beyond the count are ignored. Within one half, all column blocks c named by the block rows of one index of rows that share c // 2 are the same block.
All inputs are finite; a program needn't handle non-finite values.
Results may differ from the reference program's by a relative error of at most 0.0085.
Values may be sent and summed in bfloat16 or wider, within the bound.
No kernel may reach another device: no remote copies, remote signals or barrier semaphores. Data moves between devices by JAX's collectives and lax.ppermute only.
A program may use at most 64 MiB of HBM per device.

```python
import jax
import jax.numpy as jnp
from jax import lax

F_IN = 128
F_OUT = 256
ROWS_DEV = 256
K = 16
NODES = 4096
NBR = 64
NCB = 32
HALF_BLOCKS = 2
N_REP = 2


def draw_block_count(key, part):
    base = jax.random.fold_in(key, 11)
    key_hub, key_low, key_high = jax.random.split(base, 3)
    per_dev = ROWS_DEV // 64
    ndevs = NBR // per_dev
    hub = jax.random.randint(key_hub, (ndevs,), 0, 8) == 0
    hub = hub.at[0].set(True)
    low = jax.random.randint(key_low, (N_REP, NBR), max(1, K // 16), K // 4 + 1)
    high = jax.random.randint(key_high, (N_REP, NBR), K // 2, K + 1)
    hub_rows = jnp.repeat(hub, per_dev)[None, :]
    counts = jnp.where(hub_rows, high, low)
    counts = counts.at[:, 0].set(K)
    return counts.astype(jnp.int32)


def draw_block_cols(key, part):
    base = jax.random.fold_in(key, 23)
    key_pick, key_side = jax.random.split(base, 2)
    owners_all = NCB // HALF_BLOCKS
    per_dev = ROWS_DEV // 64
    ndevs = NBR // per_dev
    scores = jax.random.randint(key_pick, (N_REP, NBR, owners_all), 0, 1 << 20) * owners_all + jnp.arange(owners_all, dtype=jnp.int32)
    values, owners = lax.top_k(scores, K)
    sides = jax.random.randint(key_side, (N_REP, ndevs, owners_all), 0, HALF_BLOCKS)
    sides_rows = jnp.repeat(sides, per_dev, axis=1)
    within = jnp.take_along_axis(sides_rows, owners, axis=2)
    return (owners * HALF_BLOCKS + within).astype(jnp.int32)


def with_spikes(drawn, own_key, source, target, parts, factor):
    owner, partner = [(jnp.arange(drawn.shape[axis_at]) // (drawn.shape[axis_at] // parts)).reshape([-1 if axis == axis_at else 1 for axis in range(drawn.ndim)]) for axis_at in (source, target)]
    chosen = jax.random.permutation(own_key, parts)[partner]
    strong = (owner == chosen) | (owner == (partner + parts // 2) % parts)
    return jnp.where(strong, factor * drawn, drawn)


def levels(rng, shape, pieces, smallest, high):
    def one(position, shards_of):
        steps = jax.random.uniform(jax.random.fold_in(jax.random.fold_in(rng, 6), position), (shards_of,), jnp.float32, smallest / len(pieces), high / len(pieces))
        return jnp.repeat(jnp.exp(steps), shape[position] // shards_of).reshape((-1,) + (1,) * (len(shape) - position - 1))

    loudness = one(*pieces[0])
    for cut in pieces[1:]:
        loudness = loudness * one(*cut)
    return loudness


def scatter_about(own_key, shape, spread, most, shards=(), held_as=jnp.bfloat16):
    factor_of = levels(own_key, shape, shards, -0.22, 0.18) if shards else 1.0
    array = jax.random.normal(own_key, shape, jnp.float32) * spread * factor_of
    return jnp.minimum(jnp.maximum(array, -most), most).astype(held_as)


def bell_draw_with(own_key, dims, spread, limit, pieces, heavy, held_as=jnp.bfloat16):
    result = spread * jax.random.normal(own_key, dims, jnp.float32)
    if pieces:
        result = result * levels(own_key, dims, pieces, -0.22, 0.18)
    return jnp.clip(with_spikes(result, jax.random.fold_in(own_key, 3), *heavy), -limit, limit).astype(held_as)


def setup_inputs(seed: int = 0) -> dict:
    splits = jax.random.split(jax.random.key(seed), 8)
    features = scatter_about(splits[0], (NODES, F_IN), 1.0, 6.0, ((0, 16),))
    weight = scatter_about(splits[1], (F_IN, F_OUT), F_IN ** -0.5, 0.5)
    bias = scatter_about(splits[2], (F_OUT,), 0.5, 3.0, (), jnp.float32)
    block_count = draw_block_count(jax.random.fold_in(splits[7], 71), 0)
    block_cols = draw_block_cols(jax.random.fold_in(splits[7], 71), 0)
    block_vals = scatter_about(splits[5], (N_REP, NBR, K, 4096), (64 * K // 4) ** -0.5, 0.375, ((0, 2), (1, 16)))
    cotangent = bell_draw_with(splits[6], (NODES, F_OUT), (NODES ** -0.5), 0.1875, ((0, 32),), (0, 1, 32, 2.75))
    return {"features": features, "weight": weight, "bias": bias, "block_count": block_count, "block_cols": block_cols, "block_vals": block_vals, "cotangent": cotangent}


def reference(features, weight, bias, block_count, block_cols, block_vals, cotangent):
    feat_blocks = features.reshape(NBR, 64, F_IN)
    slots = jnp.arange(K, dtype=jnp.int32)

    def one_row(row):
        total = jnp.zeros((64, F_IN), jnp.float32)
        for half in range(2):
            count = block_count[half, row]
            cols = block_cols[half, row]
            index = (cols // HALF_BLOCKS) * (2 * HALF_BLOCKS) + half * HALF_BLOCKS + cols % HALF_BLOCKS
            gathered = feat_blocks[index.astype(jnp.int32)].astype(jnp.float32)
            keep = (slots < count).astype(jnp.float32)
            tiles = block_vals[half, row].reshape(K, 64, 64).astype(jnp.float32) * keep[:, None, None]
            total = total + jnp.einsum('kij,kjf->if', tiles, gathered)
        return total

    summed = lax.map(one_row, jnp.arange(NBR, dtype=jnp.int32))
    aggregated = summed.reshape(NODES, F_IN).astype(jnp.bfloat16)
    pre = jnp.dot(aggregated, weight, preferred_element_type=jnp.float32) + bias
    activated = jax.nn.silu(pre).astype(jnp.bfloat16)
    sig = jax.nn.sigmoid(pre)
    delta = (cotangent.astype(jnp.float32) * sig * (1.0 + pre * (1.0 - sig))).astype(jnp.bfloat16)
    weight_grad = jnp.dot(aggregated.T, delta, preferred_element_type=jnp.float32)
    bias_grad = jnp.sum(delta.astype(jnp.float32), axis=0)
    return activated, weight_grad, bias_grad
```

```python
import functools

import jax
import jax.numpy as jnp
from jax import lax
from jax.experimental import pallas as pl
from jax.experimental.pallas import tpu as pltpu
from jax.sharding import PartitionSpec as P

BOTH = ("rows", "rep")
VMEM = pl.BlockSpec(memory_space=pltpu.VMEM)
SMEM = pl.BlockSpec(memory_space=pltpu.SMEM)


def digit_groups(owners):
    top = owners.bit_length() - 1
    groups = []
    while top > 0:
        take = min(2, top)
        top -= take
        groups.append((top, 1 << take))
    return groups


def swap_to(value, mask, owners):
    pairs = [(i, i ^ (2 * mask + 1)) for i in range(2 * owners)]
    return lax.ppermute(value, BOTH, pairs)


def place_kernel(counts, place, vals, dense, rows):
    nblk, slots = vals.shape[0], vals.shape[1]
    wide = vals.shape[2] // 128
    dense[...] = jnp.zeros_like(dense)
    low = lax.broadcasted_iota(jnp.int32, (wide, 128), 1) < 64
    for r in range(nblk):
        for i in range(wide):
            rows[r, i * slots : (i + 1) * slots, :] = vals[r, :, i * 128 : (i + 1) * 128].astype(jnp.float32)
        for k in range(slots):

            @pl.when(k < counts[0, r])
            def _():
                here = place[r, k]
                at = here // 2
                left = here % 2 == 0
                two = rows[r, pl.ds(k, wide, stride=slots), :]
                turned = pltpu.roll(two, 64, 1)
                first = jnp.where(left, two, turned)
                second = jnp.where(left, turned, two)
                mine = low == left
                even = jnp.where(mine, first, 0.0).astype(jnp.bfloat16)
                odd = jnp.where(mine, second, 0.0).astype(jnp.bfloat16)
                dense[at, pl.ds(r * wide, wide), :] = even
                dense[at, pl.ds((nblk + r) * wide, wide), :] = odd


def place_blocks(counts, place, vals, owners):
    nblk, slots, flat = vals.shape
    wide = flat // 128
    return pl.pallas_call(
        place_kernel,
        out_shape=jax.ShapeDtypeStruct((owners, 2 * nblk * wide, 128), jnp.bfloat16),
        in_specs=[SMEM, SMEM, VMEM],
        out_specs=VMEM,
        scratch_shapes=[pltpu.VMEM((nblk, wide * slots, 128), jnp.float32)],
        name="place",
    )(counts, place, vals)


def sum_kernel(dense, feats, out):
    owners, rows, _ = dense.shape
    acc = jnp.zeros((rows, 128), jnp.float32)

    def two(q, acc):
        left = jnp.concatenate([dense[2 * q], dense[2 * q + 1]], axis=1)
        right = feats[pl.ds(pl.multiple_of(q * 256, 256), 256), :]
        return acc + jnp.dot(left, right, preferred_element_type=jnp.float32)

    if owners <= 16:
        for q in range(owners // 2):
            acc = two(q, acc)
    else:
        acc = lax.fori_loop(0, owners // 2, two, acc)
    nblk = rows // 64
    for p in range(2):
        for r in range(nblk):
            out[pl.ds(r * 64 + p, 32, stride=2), :] = acc[(p * nblk + r) * 32 : (p * nblk + r + 1) * 32]


def sum_blocks(dense, feats):
    return pl.pallas_call(
        sum_kernel,
        out_shape=jax.ShapeDtypeStruct((dense.shape[1], 128), jnp.float32),
        in_specs=[VMEM, VMEM],
        out_specs=VMEM,
        name="block_sum",
    )(dense, feats)


def layer_kernel(side, mine, other, weight, bias, cot_mine, cot_other, act, parts, value):
    half = cot_mine.shape[0]
    owners, chunk, _ = parts.shape
    share = 256 // owners
    aggregated = (mine[...] + other[...]).astype(jnp.bfloat16)
    pre = jnp.dot(aggregated, weight[...], preferred_element_type=jnp.float32) + bias[...]
    sig = 1.0 / (1.0 + jnp.exp(-pre))
    value[...] = pre * sig
    act[...] = value[pl.ds(pl.multiple_of(side[0] * half, half), half), :].astype(jnp.bfloat16)
    first = side[0] == 0
    cot_a = cot_mine[...].astype(jnp.float32)
    cot_b = cot_other[...].astype(jnp.float32)
    cot = jnp.concatenate([jnp.where(first, cot_a, cot_b), jnp.where(first, cot_b, cot_a)], axis=0)
    delta = (cot * sig * (1.0 + pre * (1.0 - sig))).astype(jnp.bfloat16)
    grad = lax.dot_general(delta, aggregated, (((0,), (0,)), ((), ())), preferred_element_type=jnp.float32)
    total = jnp.sum(delta.astype(jnp.float32), axis=0, keepdims=True)
    tail = jnp.concatenate(
        [total[:, :128], total[:, 128:], jnp.zeros((chunk - share - 2, 128), jnp.float32)], axis=0
    )
    for r in range(owners):
        parts[r] = jnp.concatenate([grad[r * share : (r + 1) * share], tail], axis=0)


def layer(side, mine, other, weight, bias, cot_mine, cot_other, owners):
    nodes = mine.shape[0]
    half, wide = cot_mine.shape
    chunk = -(-(wide // owners + 2) // 8) * 8
    return pl.pallas_call(
        layer_kernel,
        out_shape=(
            jax.ShapeDtypeStruct((half, wide), jnp.bfloat16),
            jax.ShapeDtypeStruct((owners, chunk, 128), jnp.float32),
        ),
        in_specs=[SMEM] + [VMEM] * 6,
        out_specs=(VMEM, VMEM),
        scratch_shapes=[pltpu.VMEM((nodes, wide), jnp.float32)],
        name="layer",
    )(side, mine, other, weight, bias, cot_mine, cot_other)


def finish_kernel(row, got, weight_grad, bias_grad):
    share = weight_grad.shape[0]
    total = jnp.sum(got[...], axis=0)
    weight_grad[...] = total[:share]
    flat = jnp.concatenate([total[share : share + 1], total[share + 1 : share + 2]], axis=1)
    flat = jnp.broadcast_to(flat, (8, 256))
    flat = pltpu.roll(flat, lax.rem(256 - row[0] * share, 256), 1)
    bias_grad[...] = flat[:1, :share]


def finish(row, got):
    share = 256 // got.shape[0]
    return pl.pallas_call(
        finish_kernel,
        out_shape=(
            jax.ShapeDtypeStruct((share, 128), jnp.float32),
            jax.ShapeDtypeStruct((1, share), jnp.float32),
        ),
        in_specs=[SMEM, VMEM],
        out_specs=(VMEM, VMEM),
        name="finish",
    )(row, got)


def body(features, weight, bias, block_count, block_cols, block_vals, cotangent):
    side = lax.axis_index("rep")
    row = lax.axis_index("rows")
    owners = lax.axis_size("rows")
    groups = digit_groups(owners)
    half_rows = features.shape[0] // 2

    cols = block_cols[0]
    apart = (cols // 2) ^ row
    place = jnp.zeros_like(cols)
    stride = 1
    for shift, radix in groups:
        place = place + ((apart >> shift) & (radix - 1)) * stride
        stride *= radix
    place = place * 2 + cols % 2

    flip = (len(groups) - 1) & 1
    keep = lax.dynamic_slice_in_dim(features, (side ^ flip) * half_rows, half_rows, 0)
    give = lax.dynamic_slice_in_dim(features, (1 - side ^ flip) * half_rows, half_rows, 0)
    shift, radix = groups[0]
    held = jnp.concatenate([keep] + [swap_to(give, s << shift, owners) for s in range(1, radix)])
    cot_other = swap_to(cotangent, 0, owners)
    for shift, radix in groups[1:]:
        held = jnp.concatenate([swap_to(held, s << shift, owners) for s in range(radix)])

    dense = place_blocks(block_count, place, block_vals[0], owners)
    mine = sum_blocks(dense, held)
    other = swap_to(mine, 0, owners)
    side_arr = side.reshape(1).astype(jnp.int32)
    activated, parts = layer(
        side_arr, mine, other, weight, bias.reshape(1, -1), cotangent, cot_other, owners
    )
    got = lax.all_to_all(parts, "rows", split_axis=0, concat_axis=0, tiled=True)
    weight_grad, bias_grad = finish(row.reshape(1).astype(jnp.int32), got)
    return activated, weight_grad.T, bias_grad.reshape(-1)


def solution(mesh):
    placed = (
        P("rows", None),
        P(),
        P(),
        P("rep", "rows"),
        P("rep", "rows", None),
        P("rep", "rows", None, None),
        P(BOTH, None),
    )
    return jax.shard_map(
        body,
        mesh=mesh,
        in_specs=placed,
        out_specs=(P(BOTH, None), P(None, "rows"), P("rows")),
        check_vma=False,
    )
```

```python
import functools

import functools

import jax
import jax.numpy as jnp
from jax import lax
from jax.experimental import pallas as pl
from jax.experimental.pallas import tpu as pltpu
from jax.sharding import PartitionSpec as P

BOTH = ("rows", "rep")
VMEM = pl.BlockSpec(memory_space=pltpu.VMEM)
SMEM = pl.BlockSpec(memory_space=pltpu.SMEM)


def digit_groups(owners):
    top = owners.bit_length() - 1
    groups = []
    while top > 0:
        take = min(2, top)
        top -= take
        groups.append((top, 1 << take))
    return groups


def swap_to(value, mask, owners):
    pairs = [(i, i ^ (2 * mask + 1)) for i in range(2 * owners)]
    return lax.ppermute(value, BOTH, pairs)


def limit(owners):
    return pltpu.CompilerParams(vmem_limit_bytes=(8 if owners <= 16 else 48) << 20)


def place_kernel(groups, row, counts, cols, vals, dense):
    nblk, slots, flat = vals.shape
    owners = dense.shape[0]
    wide = flat // 128
    deep = 16 * slots
    lane = lax.broadcasted_iota(jnp.int32, (slots, deep), 1)
    slot = lax.broadcasted_iota(jnp.int32, (slots, deep), 0)
    spread = (lane % slots == slot).astype(jnp.bfloat16)
    named = jnp.dot(cols[...].astype(jnp.bfloat16), spread, preferred_element_type=jnp.float32)
    named = named.astype(jnp.int32)
    apart = (named >> 1) ^ row[0]
    place = jnp.zeros_like(apart)
    stride = 1
    for shift, radix in groups:
        place = place + ((apart >> shift) & (radix - 1)) * stride
        stride *= radix
    side = named & 1
    lane = lax.broadcasted_iota(jnp.int32, (1, deep), 1)
    at = lax.broadcasted_iota(jnp.int32, (256, deep), 0)
    same = at % 16 == lax.broadcasted_iota(jnp.int32, (256, deep), 1) // slots
    low = lax.broadcasted_iota(jnp.int32, (slots, 128), 1) < 64
    for r in range(nblk):
        used = lane % slots < counts[0, r]
        to_first = jnp.where(used & (side[r : r + 1] == 0), place[r : r + 1], -1)
        to_second = jnp.where(used & (side[r : r + 1] == 1), place[r : r + 1], -1)
        rights = []
        for g in range(wide // 16):
            top, bottom = [], []
            for i in range(g * 16, g * 16 + 16):
                two = vals[r, :, i * 128 : (i + 1) * 128].astype(jnp.float32)
                turned = pltpu.roll(two, 64, 1)
                top.append(jnp.concatenate([jnp.where(low, two, 0.0), jnp.where(low, turned, 0.0)], axis=1).astype(jnp.bfloat16))
                bottom.append(jnp.concatenate([jnp.where(low, 0.0, turned), jnp.where(low, 0.0, two)], axis=1).astype(jnp.bfloat16))
            rights.append(jnp.concatenate(top + bottom, axis=0))

        def put(q):
            here = at // 16 + q * 16
            pick = jnp.concatenate([same & (here == to_first), same & (here == to_second)], axis=1)
            pick = pick.astype(jnp.bfloat16)
            for g, right in enumerate(rights):
                moved = jnp.dot(pick, right, preferred_element_type=jnp.float32).astype(jnp.bfloat16)
                moved = moved.reshape(16, 16, 256)
                start = r * wide + g * 16
                dense[pl.ds(q * 16, 16), start : start + 16, :] = moved[:, :, :128]
                start += nblk * wide
                dense[pl.ds(q * 16, 16), start : start + 16, :] = moved[:, :, 128:]

        if owners <= 16:
            put(0)
        else:
            pl.loop(0, owners // 16)(put)


def place_blocks(row, counts, cols, vals, owners):
    nblk, slots, flat = vals.shape
    wide = flat // 128
    return pl.pallas_call(
        functools.partial(place_kernel, digit_groups(owners)),
        out_shape=jax.ShapeDtypeStruct((owners, 2 * nblk * wide, 128), jnp.bfloat16),
        in_specs=[SMEM, SMEM, VMEM, VMEM],
        out_specs=VMEM,
        compiler_params=limit(owners),
        name="place",
    )(row, counts, cols, vals)


def sum_kernel(dense, *refs):
    pieces, out = refs[:-1], refs[-1]
    owners, rows, _ = dense.shape
    each = owners // len(pieces)
    acc = jnp.zeros((rows, 128), jnp.float32)
    for s, feats in enumerate(pieces):

        def two(q, acc):
            at = s * each + 2 * q
            left = jnp.concatenate([dense[at], dense[at + 1]], axis=1)
            right = feats[pl.ds(pl.multiple_of(q * 256, 256), 256), :]
            return acc + jnp.dot(left, right, preferred_element_type=jnp.float32)

        if each <= 16:
            for q in range(each // 2):
                acc = two(q, acc)
        else:
            acc = lax.fori_loop(0, each // 2, two, acc)
    nblk = rows // 64
    for p in range(2):
        for r in range(nblk):
            out[pl.ds(r * 64 + p, 32, stride=2), :] = acc[(p * nblk + r) * 32 : (p * nblk + r + 1) * 32]


def sum_blocks(dense, pieces):
    return pl.pallas_call(
        sum_kernel,
        out_shape=jax.ShapeDtypeStruct((dense.shape[1], 128), jnp.float32),
        in_specs=[VMEM] * (1 + len(pieces)),
        out_specs=VMEM,
        compiler_params=limit(dense.shape[0]),
        name="block_sum",
    )(dense, *pieces)


def layer_kernel(side, mine, other, weight, bias, cot_mine, cot_other, act, parts, value):
    half = cot_mine.shape[0]
    owners, chunk, _ = parts.shape
    share = 256 // owners
    aggregated = (mine[...] + other[...]).astype(jnp.bfloat16)
    pre = jnp.dot(aggregated, weight[...], preferred_element_type=jnp.float32) + bias[...]
    sig = 1.0 / (1.0 + jnp.exp(-pre))
    value[...] = pre * sig
    act[...] = value[pl.ds(pl.multiple_of(side[0] * half, half), half), :].astype(jnp.bfloat16)
    first = side[0] == 0
    cot_a = cot_mine[...].astype(jnp.float32)
    cot_b = cot_other[...].astype(jnp.float32)
    cot = jnp.concatenate([jnp.where(first, cot_a, cot_b), jnp.where(first, cot_b, cot_a)], axis=0)
    delta = (cot * sig * (1.0 + pre * (1.0 - sig))).astype(jnp.bfloat16)
    grad = lax.dot_general(delta, aggregated, (((0,), (0,)), ((), ())), preferred_element_type=jnp.float32)
    total = jnp.sum(delta.astype(jnp.float32), axis=0, keepdims=True)
    tail = jnp.concatenate(
        [total[:, :128], total[:, 128:], jnp.zeros((chunk - share - 2, 128), jnp.float32)], axis=0
    )
    for r in range(owners):
        parts[r] = jnp.concatenate([grad[r * share : (r + 1) * share], tail], axis=0)


def layer(side, mine, other, weight, bias, cot_mine, cot_other, owners):
    nodes = mine.shape[0]
    half, wide = cot_mine.shape
    chunk = -(-(wide // owners + 2) // 8) * 8
    return pl.pallas_call(
        layer_kernel,
        out_shape=(
            jax.ShapeDtypeStruct((half, wide), jnp.bfloat16),
            jax.ShapeDtypeStruct((owners, chunk, 128), jnp.float32),
        ),
        in_specs=[SMEM] + [VMEM] * 6,
        out_specs=(VMEM, VMEM),
        scratch_shapes=[pltpu.VMEM((nodes, wide), jnp.float32)],
        compiler_params=limit(owners),
        name="layer",
    )(side, mine, other, weight, bias, cot_mine, cot_other)


def finish_kernel(row, got, weight_grad, bias_grad):
    share = weight_grad.shape[0]
    total = jnp.sum(got[...], axis=0)
    weight_grad[...] = total[:share]
    flat = jnp.concatenate([total[share : share + 1], total[share + 1 : share + 2]], axis=1)
    flat = jnp.broadcast_to(flat, (8, 256))
    flat = pltpu.roll(flat, lax.rem(256 - row[0] * share, 256), 1)
    bias_grad[...] = flat[:1, :share]


def finish(row, got):
    share = 256 // got.shape[0]
    return pl.pallas_call(
        finish_kernel,
        out_shape=(
            jax.ShapeDtypeStruct((share, 128), jnp.float32),
            jax.ShapeDtypeStruct((1, share), jnp.float32),
        ),
        in_specs=[SMEM, VMEM],
        out_specs=(VMEM, VMEM),
        compiler_params=limit(got.shape[0]),
        name="finish",
    )(row, got)


def body(features, weight, bias, block_count, block_cols, block_vals, cotangent):
    side = lax.axis_index("rep")
    row = lax.axis_index("rows")
    owners = lax.axis_size("rows")
    groups = digit_groups(owners)
    half_rows = features.shape[0] // 2

    row_arr = row.reshape(1).astype(jnp.int32)
    dense = place_blocks(row_arr, block_count, block_cols[0], block_vals[0], owners)

    flip = (len(groups) - 1) & 1
    keep = lax.dynamic_slice_in_dim(features, (side ^ flip) * half_rows, half_rows, 0)
    give = lax.dynamic_slice_in_dim(features, (1 - side ^ flip) * half_rows, half_rows, 0)
    shift, radix = groups[0]
    pieces = [keep] + [swap_to(give, s << shift, owners) for s in range(1, radix)]
    cot_other = swap_to(cotangent, 0, owners)
    for shift, radix in groups[1:]:
        held, dense, cot_other = lax.optimization_barrier((jnp.concatenate(pieces), dense, cot_other))
        pieces = [swap_to(held, s << shift, owners) for s in range(radix)]

    mine = sum_blocks(dense, pieces)
    other = swap_to(mine, 0, owners)
    side_arr = side.reshape(1).astype(jnp.int32)
    activated, parts = layer(
        side_arr, mine, other, weight, bias.reshape(1, -1), cotangent, cot_other, owners
    )
    got = lax.all_to_all(parts, "rows", split_axis=0, concat_axis=0, tiled=True)
    weight_grad, bias_grad = finish(row_arr, got)
    return activated, weight_grad.T, bias_grad.reshape(-1)


def solution(mesh):
    placed = (
        P("rows", None),
        P(),
        P(),
        P("rep", "rows"),
        P("rep", "rows", None),
        P("rep", "rows", None, None),
        P(BOTH, None),
    )
    return jax.shard_map(
        body,
        mesh=mesh,
        in_specs=placed,
        out_specs=(P(BOTH, None), P(None, "rows"), P("rows")),
        check_vma=False,
    )
```

```python
import functools

import functools

import jax
import jax.numpy as jnp
from jax import lax
from jax.experimental import pallas as pl
from jax.experimental.pallas import tpu as pltpu
from jax.sharding import PartitionSpec as P

BOTH = ("rows", "rep")
VMEM = pl.BlockSpec(memory_space=pltpu.VMEM)
SMEM = pl.BlockSpec(memory_space=pltpu.SMEM)


def digit_groups(owners):
    top = owners.bit_length() - 1
    groups = []
    while top > 0:
        take = min(2, top)
        top -= take
        groups.append((top, 1 << take))
    return groups


def across(value, mask, owners, swap):
    pairs = [(i, i ^ (2 * mask + swap)) for i in range(2 * owners)]
    return lax.ppermute(value, BOTH, pairs)


def limit(owners):
    return pltpu.CompilerParams(vmem_limit_bytes=(8 if owners <= 16 else 48) << 20)


def place_kernel(groups, index, counts, cols, vals, cot, weight, bias, dense, cot_out, weight_out, bias_out):
    nblk, slots, flat = vals.shape
    owners = dense.shape[0]
    cot_out[...] = cot[...]
    weight_out[...] = weight[...]
    bias_out[...] = bias[...]
    wide = flat // 128
    deep = 16 * slots
    lane = lax.broadcasted_iota(jnp.int32, (slots, deep), 1)
    slot = lax.broadcasted_iota(jnp.int32, (slots, deep), 0)
    spread = (lane % slots == slot).astype(jnp.bfloat16)
    named = jnp.dot(cols[...].astype(jnp.bfloat16), spread, preferred_element_type=jnp.float32)
    named = named.astype(jnp.int32)
    apart = (named >> 1) ^ (index[0] >> 1)
    place = jnp.zeros_like(apart)
    stride = 1
    for shift, radix in groups:
        place = place + ((apart >> shift) & (radix - 1)) * stride
        stride *= radix
    side = named & 1
    lane = lax.broadcasted_iota(jnp.int32, (1, deep), 1)
    at = lax.broadcasted_iota(jnp.int32, (256, deep), 0)
    same = at % 16 == lax.broadcasted_iota(jnp.int32, (256, deep), 1) // slots
    low = lax.broadcasted_iota(jnp.int32, (slots, 128), 1) < 64
    for r in range(nblk):
        used = lane % slots < counts[0, r]
        to_first = jnp.where(used & (side[r : r + 1] == 0), place[r : r + 1], -1)
        to_second = jnp.where(used & (side[r : r + 1] == 1), place[r : r + 1], -1)
        rights = []
        for g in range(wide // 16):
            top, bottom = [], []
            for i in range(g * 16, g * 16 + 16):
                two = vals[r, :, i * 128 : (i + 1) * 128].astype(jnp.float32)
                turned = pltpu.roll(two, 64, 1)
                top.append(jnp.concatenate([jnp.where(low, two, 0.0), jnp.where(low, turned, 0.0)], axis=1).astype(jnp.bfloat16))
                bottom.append(jnp.concatenate([jnp.where(low, 0.0, turned), jnp.where(low, 0.0, two)], axis=1).astype(jnp.bfloat16))
            rights.append(jnp.concatenate(top + bottom, axis=0))

        def put(q):
            here = at // 16 + q * 16
            pick = jnp.concatenate([same & (here == to_first), same & (here == to_second)], axis=1)
            pick = pick.astype(jnp.bfloat16)
            for g, right in enumerate(rights):
                moved = jnp.dot(pick, right, preferred_element_type=jnp.float32).astype(jnp.bfloat16)
                moved = moved.reshape(16, 16, 256)
                start = r * wide + g * 16
                dense[pl.ds(q * 16, 16), start : start + 16, :] = moved[:, :, :128]
                start += nblk * wide
                dense[pl.ds(q * 16, 16), start : start + 16, :] = moved[:, :, 128:]

        if owners <= 16:
            put(0)
        else:
            pl.loop(0, owners // 16)(put)


def place_blocks(index, counts, cols, vals, cot, weight, bias, owners):
    nblk, slots, flat = vals.shape
    wide = flat // 128
    return pl.pallas_call(
        functools.partial(place_kernel, digit_groups(owners)),
        out_shape=(
            jax.ShapeDtypeStruct((owners, 2 * nblk * wide, 128), jnp.bfloat16),
            jax.ShapeDtypeStruct(cot.shape, cot.dtype),
            jax.ShapeDtypeStruct(weight.shape, weight.dtype),
            jax.ShapeDtypeStruct(bias.shape, bias.dtype),
        ),
        in_specs=[SMEM, SMEM] + [VMEM] * 5,
        out_specs=(VMEM,) * 4,
        compiler_params=limit(owners),
        name="place",
    )(index, counts, cols, vals, cot, weight, bias)


def sum_kernel(dense, *refs):
    pieces, out = refs[:-1], refs[-1]
    owners, rows, _ = dense.shape
    each = owners // len(pieces)
    acc = jnp.zeros((rows, 128), jnp.float32)
    for s, feats in enumerate(pieces):

        def two(q, acc):
            at = s * each + 2 * q
            left = jnp.concatenate([dense[at], dense[at + 1]], axis=1)
            right = feats[pl.ds(pl.multiple_of(q * 256, 256), 256), :]
            return acc + jnp.dot(left, right, preferred_element_type=jnp.float32)

        if each <= 16:
            for q in range(each // 2):
                acc = two(q, acc)
        else:
            acc = lax.fori_loop(0, each // 2, two, acc)
    nblk = rows // 64
    for p in range(2):
        for r in range(nblk):
            out[pl.ds(r * 64 + p, 32, stride=2), :] = acc[(p * nblk + r) * 32 : (p * nblk + r + 1) * 32]


def sum_blocks(dense, pieces):
    return pl.pallas_call(
        sum_kernel,
        out_shape=jax.ShapeDtypeStruct((dense.shape[1], 128), jnp.float32),
        in_specs=[VMEM] * (1 + len(pieces)),
        out_specs=VMEM,
        compiler_params=limit(dense.shape[0]),
        name="block_sum",
    )(dense, *pieces)


def layer_kernel(index, mine, other, weight, bias, cot_mine, cot_other, act, parts, value):
    half = cot_mine.shape[0]
    side = index[0] & 1
    owners, chunk, _ = parts.shape
    share = 256 // owners
    aggregated = (mine[...] + other[...]).astype(jnp.bfloat16)
    pre = jnp.dot(aggregated, weight[...], preferred_element_type=jnp.float32) + bias[...]
    sig = 1.0 / (1.0 + jnp.exp(-pre))
    value[...] = pre * sig
    act[...] = value[pl.ds(pl.multiple_of(side * half, half), half), :].astype(jnp.bfloat16)
    first = side == 0
    cot_a = cot_mine[...].astype(jnp.float32)
    cot_b = cot_other[...].astype(jnp.float32)
    cot = jnp.concatenate([jnp.where(first, cot_a, cot_b), jnp.where(first, cot_b, cot_a)], axis=0)
    delta = (cot * sig * (1.0 + pre * (1.0 - sig))).astype(jnp.bfloat16)
    grad = lax.dot_general(delta, aggregated, (((0,), (0,)), ((), ())), preferred_element_type=jnp.float32)
    total = jnp.sum(delta.astype(jnp.float32), axis=0, keepdims=True)
    tail = jnp.concatenate(
        [total[:, :128], total[:, 128:], jnp.zeros((chunk - share - 2, 128), jnp.float32)], axis=0
    )
    for r in range(owners):
        parts[r] = jnp.concatenate([grad[r * share : (r + 1) * share], tail], axis=0)


def layer(index, mine, other, weight, bias, cot_mine, cot_other, owners):
    nodes = mine.shape[0]
    half, wide = cot_mine.shape
    chunk = -(-(wide // owners + 2) // 8) * 8
    return pl.pallas_call(
        layer_kernel,
        out_shape=(
            jax.ShapeDtypeStruct((half, wide), jnp.bfloat16),
            jax.ShapeDtypeStruct((owners, chunk, 128), jnp.float32),
        ),
        in_specs=[SMEM] + [VMEM] * 6,
        out_specs=(VMEM, VMEM),
        scratch_shapes=[pltpu.VMEM((nodes, wide), jnp.float32)],
        compiler_params=limit(owners),
        name="layer",
    )(index, mine, other, weight, bias, cot_mine, cot_other)


def finish_kernel(index, got, weight_grad, bias_grad):
    share = weight_grad.shape[0]
    total = jnp.sum(got[...], axis=0)
    weight_grad[...] = total[:share]
    flat = jnp.concatenate([total[share : share + 1], total[share + 1 : share + 2]], axis=1)
    flat = jnp.broadcast_to(flat, (8, 256))
    flat = pltpu.roll(flat, lax.rem(256 - (index[0] >> 1) * share, 256), 1)
    bias_grad[...] = flat[:1, :share]


def finish(index, got):
    share = 256 // got.shape[0]
    return pl.pallas_call(
        finish_kernel,
        out_shape=(
            jax.ShapeDtypeStruct((share, 128), jnp.float32),
            jax.ShapeDtypeStruct((1, share), jnp.float32),
        ),
        in_specs=[SMEM, VMEM],
        out_specs=(VMEM, VMEM),
        compiler_params=limit(got.shape[0]),
        name="finish",
    )(index, got)


def body(features, weight, bias, block_count, block_cols, block_vals, cotangent):
    side = lax.axis_index("rep")
    owners = lax.axis_size("rows")
    groups = digit_groups(owners)
    half_rows = features.shape[0] // 2

    keep = lax.dynamic_slice_in_dim(features, side * half_rows, half_rows, 0)
    give = lax.dynamic_slice_in_dim(features, (1 - side) * half_rows, half_rows, 0)
    shift, radix = groups[0]
    pieces = [keep] + [across(give, s << shift, owners, 1) for s in range(1, radix)]
    vals = block_vals[0]
    for shift, radix in groups[1:]:
        held, vals = lax.optimization_barrier((jnp.concatenate(pieces), vals))
        pieces = [held] + [across(held, s << shift, owners, 0) for s in range(1, radix)]

    index = lax.axis_index(BOTH).reshape(1).astype(jnp.int32)
    dense, cot_mine, weight, bias = place_blocks(
        index, block_count, block_cols[0], vals, cotangent, weight, bias.reshape(1, -1), owners
    )
    cot_other = across(cot_mine, 0, owners, 1)
    dense, cot_other = lax.optimization_barrier((dense, cot_other))

    mine = sum_blocks(dense, pieces)
    other = across(mine, 0, owners, 1)
    activated, parts = layer(index, mine, other, weight, bias, cot_mine, cot_other, owners)
    got = lax.all_to_all(parts, "rows", split_axis=0, concat_axis=0, tiled=True)
    weight_grad, bias_grad = finish(index, got)
    return activated, weight_grad.T, bias_grad.reshape(-1)


def solution(mesh):
    placed = (
        P("rows", None),
        P(),
        P(),
        P("rep", "rows"),
        P("rep", "rows", None),
        P("rep", "rows", None, None),
        P(BOTH, None),
    )
    return jax.shard_map(
        body,
        mesh=mesh,
        in_specs=placed,
        out_specs=(P(BOTH, None), P(None, "rows"), P("rows")),
        check_vma=False,
    )
```

```python
import functools

import functools

import jax
import jax.numpy as jnp
from jax import lax
from jax.experimental import pallas as pl
from jax.experimental.pallas import tpu as pltpu
from jax.sharding import PartitionSpec as P

BOTH = ("rows", "rep")
VMEM = pl.BlockSpec(memory_space=pltpu.VMEM)
SMEM = pl.BlockSpec(memory_space=pltpu.SMEM)


def digit_groups(owners):
    top = owners.bit_length() - 1
    groups = []
    while top > 0:
        take = min(2, top)
        top -= take
        groups.append((top, 1 << take))
    return groups


def across(value, mask, owners, swap):
    pairs = [(i, i ^ (2 * mask + swap)) for i in range(2 * owners)]
    return lax.ppermute(value, BOTH, pairs)


def limit(owners):
    return pltpu.CompilerParams(vmem_limit_bytes=(8 if owners <= 16 else 48) << 20)


def place_kernel(groups, counts, cols, vals, cot, weight, bias, dense, cot_out, weight_out, bias_out):
    nblk, slots, flat = vals.shape
    owners = dense.shape[0]
    cot_out[...] = cot[...].astype(jnp.float32).T.astype(jnp.bfloat16)
    weight_out[...] = weight[...].astype(jnp.float32).T.astype(jnp.bfloat16)
    bias_out[...] = jnp.broadcast_to(bias[...], (128, bias.shape[1])).T
    wide = flat // 128
    deep = 16 * slots
    lane = lax.broadcasted_iota(jnp.int32, (slots, deep), 1)
    slot = lax.broadcasted_iota(jnp.int32, (slots, deep), 0)
    spread = (lane % slots == slot).astype(jnp.bfloat16)
    named = jnp.dot(cols[...].astype(jnp.bfloat16), spread, preferred_element_type=jnp.float32)
    named = named.astype(jnp.int32)
    apart = (named >> 1) ^ lax.axis_index("rows")
    place = jnp.zeros_like(apart)
    stride = 1
    for shift, radix in groups:
        place = place + ((apart >> shift) & (radix - 1)) * stride
        stride *= radix
    side = named & 1
    lane = lax.broadcasted_iota(jnp.int32, (1, deep), 1)
    at = lax.broadcasted_iota(jnp.int32, (256, deep), 0)
    same = at % 16 == lax.broadcasted_iota(jnp.int32, (256, deep), 1) // slots
    low = lax.broadcasted_iota(jnp.int32, (slots, 128), 1) < 64
    for r in range(nblk):
        used = lane % slots < counts[0, r]
        to_first = jnp.where(used & (side[r : r + 1] == 0), place[r : r + 1], -1)
        to_second = jnp.where(used & (side[r : r + 1] == 1), place[r : r + 1], -1)
        rights = []
        for g in range(wide // 16):
            top, bottom = [], []
            for i in range(g * 16, g * 16 + 16):
                two = vals[r, :, i * 128 : (i + 1) * 128].astype(jnp.float32)
                turned = pltpu.roll(two, 64, 1)
                top.append(jnp.concatenate([jnp.where(low, two, 0.0), jnp.where(low, turned, 0.0)], axis=1).astype(jnp.bfloat16))
                bottom.append(jnp.concatenate([jnp.where(low, 0.0, turned), jnp.where(low, 0.0, two)], axis=1).astype(jnp.bfloat16))
            rights.append(jnp.concatenate(top + bottom, axis=0))

        def put(q):
            here = at // 16 + q * 16
            pick = jnp.concatenate([same & (here == to_first), same & (here == to_second)], axis=1)
            pick = pick.astype(jnp.bfloat16)
            for g, right in enumerate(rights):
                moved = jnp.dot(pick, right, preferred_element_type=jnp.float32).astype(jnp.bfloat16)
                moved = moved.reshape(16, 16, 256)
                start = r * wide + g * 16
                dense[pl.ds(q * 16, 16), start : start + 16, :] = moved[:, :, :128]
                start += nblk * wide
                dense[pl.ds(q * 16, 16), start : start + 16, :] = moved[:, :, 128:]

        if owners <= 16:
            put(0)
        else:
            pl.loop(0, owners // 16)(put)


def place_blocks(counts, cols, vals, cot, weight, bias, owners):
    nblk, slots, flat = vals.shape
    wide = flat // 128
    return pl.pallas_call(
        functools.partial(place_kernel, digit_groups(owners)),
        out_shape=(
            jax.ShapeDtypeStruct((owners, 2 * nblk * wide, 128), jnp.bfloat16),
            jax.ShapeDtypeStruct(cot.shape[::-1], cot.dtype),
            jax.ShapeDtypeStruct(weight.shape[::-1], weight.dtype),
            jax.ShapeDtypeStruct((bias.shape[1], 128), bias.dtype),
        ),
        in_specs=[SMEM] + [VMEM] * 5,
        out_specs=(VMEM,) * 4,
        compiler_params=limit(owners),
        name="place",
    )(counts, cols, vals, cot, weight, bias)


def sum_kernel(dense, *refs):
    pieces, out = refs[:-1], refs[-1]
    owners, rows, _ = dense.shape
    each = owners // len(pieces)
    acc = jnp.zeros((rows, 128), jnp.float32)
    for s, feats in enumerate(pieces):

        def two(q, acc):
            at = s * each + 2 * q
            left = jnp.concatenate([dense[at], dense[at + 1]], axis=1)
            right = feats[pl.ds(pl.multiple_of(q * 256, 256), 256), :]
            return acc + jnp.dot(left, right, preferred_element_type=jnp.float32)

        if each <= 16:
            for q in range(each // 2):
                acc = two(q, acc)
        else:
            acc = lax.fori_loop(0, each // 2, two, acc)
    nblk = rows // 64
    for p in range(2):
        for r in range(nblk):
            out[pl.ds(r * 64 + p, 32, stride=2), :] = acc[(p * nblk + r) * 32 : (p * nblk + r + 1) * 32]


def sum_blocks(dense, pieces):
    return pl.pallas_call(
        sum_kernel,
        out_shape=jax.ShapeDtypeStruct((dense.shape[1], 128), jnp.float32),
        in_specs=[VMEM] * (1 + len(pieces)),
        out_specs=VMEM,
        compiler_params=limit(dense.shape[0]),
        name="block_sum",
    )(dense, *pieces)


NT = (((1,), (1,)), ((), ()))


def layer_kernel(mine, other, weight_t, bias_t, cot_mine, cot_other, parts):
    first = lax.axis_index("rep") == 0
    owners, chunk, _ = parts.shape
    share = weight_t.shape[0] // owners
    aggregated = (mine[...] + other[...]).astype(jnp.bfloat16)
    pre = lax.dot_general(weight_t[...], aggregated, NT, preferred_element_type=jnp.float32)
    pre = pre + jnp.concatenate([bias_t[...]] * (pre.shape[1] // 128), axis=1)
    sig = 1.0 / (1.0 + jnp.exp(-pre))
    cot_a, cot_b = cot_mine[...].astype(jnp.float32), cot_other[...].astype(jnp.float32)
    cot = jnp.concatenate([jnp.where(first, cot_a, cot_b), jnp.where(first, cot_b, cot_a)], axis=1)
    delta = (cot * sig * (1.0 + pre * (1.0 - sig))).astype(jnp.bfloat16)
    grad = jnp.dot(delta, aggregated, preferred_element_type=jnp.float32)
    ones = jnp.ones((16, delta.shape[1]), jnp.bfloat16)
    total = lax.dot_general(ones, delta, NT, preferred_element_type=jnp.float32)[:1]
    blank = jnp.zeros((chunk - share - 2, 128), jnp.float32)
    tail = jnp.concatenate([total[:, :128], total[:, 128:], blank], axis=0)
    for r in range(owners):
        parts[r] = jnp.concatenate([grad[r * share : (r + 1) * share], tail], axis=0).astype(parts.dtype)


def layer(mine, other, weight_t, bias_t, cot_mine, cot_other, owners):
    share = weight_t.shape[0] // owners
    chunk = -(-(share + 2) // 8) * 8
    return pl.pallas_call(
        layer_kernel,
        out_shape=jax.ShapeDtypeStruct((owners, chunk, 128), jnp.float32),
        in_specs=[VMEM] * 6,
        out_specs=VMEM,
        compiler_params=limit(owners),
        name="layer",
    )(mine, other, weight_t, bias_t, cot_mine, cot_other)


def finish_kernel(mine, other, weight, bias, got, act, weight_grad, bias_grad):
    half = act.shape[0]
    own = pl.ds(pl.multiple_of(lax.axis_index("rep") * half, half), half)
    aggregated = (mine[own, :] + other[own, :]).astype(jnp.bfloat16)
    pre = jnp.dot(aggregated, weight[...], preferred_element_type=jnp.float32) + bias[...]
    act[...] = (pre / (1.0 + jnp.exp(-pre))).astype(act.dtype)
    share = weight_grad.shape[0]
    total = jnp.sum(got[...], axis=0)
    weight_grad[...] = total[:share]
    flat = jnp.concatenate([total[share : share + 1], total[share + 1 : share + 2]], axis=1)
    flat = jnp.broadcast_to(flat, (8, 256))
    flat = pltpu.roll(flat, lax.rem(256 - lax.axis_index("rows") * share, 256), 1)
    bias_grad[...] = flat[:1, :share]


def finish(mine, other, weight, bias, got):
    owners = got.shape[0]
    share = weight.shape[1] // owners
    return pl.pallas_call(
        finish_kernel,
        out_shape=(
            jax.ShapeDtypeStruct((mine.shape[0] // 2, weight.shape[1]), jnp.bfloat16),
            jax.ShapeDtypeStruct((share, 128), jnp.float32),
            jax.ShapeDtypeStruct((1, share), jnp.float32),
        ),
        in_specs=[VMEM] * 5,
        out_specs=(VMEM,) * 3,
        compiler_params=limit(owners),
        name="finish",
    )(mine, other, weight, bias, got)


def body(features, weight, bias, block_count, block_cols, block_vals, cotangent):
    side = lax.axis_index("rep")
    owners = lax.axis_size("rows")
    groups = digit_groups(owners)
    half_rows = features.shape[0] // 2

    keep = lax.dynamic_slice_in_dim(features, side * half_rows, half_rows, 0)
    give = lax.dynamic_slice_in_dim(features, (1 - side) * half_rows, half_rows, 0)
    shift, radix = groups[0]
    pieces = [keep] + [across(give, s << shift, owners, 1) for s in range(1, radix)]
    vals = block_vals[0]
    for shift, radix in groups[1:]:
        held, vals = lax.optimization_barrier((jnp.concatenate(pieces), vals))
        pieces = [held] + [across(held, s << shift, owners, 0) for s in range(1, radix)]

    bias = bias.reshape(1, -1)
    dense, cot_mine, weight_t, bias_t = place_blocks(
        block_count, block_cols[0], vals, cotangent, weight, bias, owners
    )
    cot_other = across(cot_mine, 0, owners, 1)
    dense, cot_other = lax.optimization_barrier((dense, cot_other))

    mine = sum_blocks(dense, pieces)
    other = across(mine, 0, owners, 1)
    parts = layer(mine, other, weight_t, bias_t, cot_mine, cot_other, owners)
    got = lax.all_to_all(parts, "rows", split_axis=0, concat_axis=0, tiled=True)
    activated, weight_grad, bias_grad = finish(mine, other, weight, bias, got)
    return activated, weight_grad.T, bias_grad.reshape(-1)


def solution(mesh):
    placed = (
        P("rows", None),
        P(),
        P(),
        P("rep", "rows"),
        P("rep", "rows", None),
        P("rep", "rows", None, None),
        P(BOTH, None),
    )
    return jax.shard_map(
        body,
        mesh=mesh,
        in_specs=placed,
        out_specs=(P(BOTH, None), P(None, "rows"), P("rows")),
        check_vma=False,
    )
```

```python
import functools

import functools

import jax
import jax.numpy as jnp
from jax import lax
from jax.experimental import pallas as pl
from jax.experimental.pallas import tpu as pltpu
from jax.sharding import PartitionSpec as P

BOTH = ("rows", "rep")
VMEM = pl.BlockSpec(memory_space=pltpu.VMEM)
SMEM = pl.BlockSpec(memory_space=pltpu.SMEM)


def digit_groups(owners):
    top = owners.bit_length() - 1
    groups = []
    while top > 0:
        take = min(2, top)
        top -= take
        groups.append((top, 1 << take))
    return groups


def across(value, mask, owners, swap):
    pairs = [(i, i ^ (2 * mask + swap)) for i in range(2 * owners)]
    return lax.ppermute(value, BOTH, pairs)


def limit(owners):
    return pltpu.CompilerParams(vmem_limit_bytes=(8 if owners <= 16 else 48) << 20)


def place_kernel(groups, counts, cols, vals, cot, weight, bias, dense, cot_out, weight_out, bias_out):
    nblk, slots, flat = vals.shape
    owners = dense.shape[0]
    cot_out[...] = cot[...].astype(jnp.float32).T.astype(jnp.bfloat16)
    weight_out[...] = weight[...].astype(jnp.float32).T.astype(jnp.bfloat16)
    bias_out[...] = jnp.broadcast_to(bias[...], (128, bias.shape[1])).T
    wide = flat // 128
    deep = 16 * slots
    lane = lax.broadcasted_iota(jnp.int32, (slots, deep), 1)
    slot = lax.broadcasted_iota(jnp.int32, (slots, deep), 0)
    spread = (lane % slots == slot).astype(jnp.bfloat16)
    named = jnp.dot(cols[...].astype(jnp.bfloat16), spread, preferred_element_type=jnp.float32)
    named = named.astype(jnp.int32)
    apart = (named >> 1) ^ lax.axis_index("rows")
    place = jnp.zeros_like(apart)
    stride = 1
    for shift, radix in groups:
        place = place + ((apart >> shift) & (radix - 1)) * stride
        stride *= radix
    side = named & 1
    lane = lax.broadcasted_iota(jnp.int32, (1, deep), 1)
    at = lax.broadcasted_iota(jnp.int32, (256, deep), 0)
    same = at % 16 == lax.broadcasted_iota(jnp.int32, (256, deep), 1) // slots
    low = lax.broadcasted_iota(jnp.int32, (slots, 128), 1) < 64
    for r in range(nblk):
        used = lane % slots < counts[0, r]
        to_first = jnp.where(used & (side[r : r + 1] == 0), place[r : r + 1], -1)
        to_second = jnp.where(used & (side[r : r + 1] == 1), place[r : r + 1], -1)
        rights = []
        for g in range(wide // 16):
            top, bottom = [], []
            for i in range(g * 16, g * 16 + 16):
                two = vals[r, :, i * 128 : (i + 1) * 128].astype(jnp.float32)
                turned = pltpu.roll(two, 64, 1)
                top.append(jnp.concatenate([jnp.where(low, two, 0.0), jnp.where(low, turned, 0.0)], axis=1).astype(jnp.bfloat16))
                bottom.append(jnp.concatenate([jnp.where(low, 0.0, turned), jnp.where(low, 0.0, two)], axis=1).astype(jnp.bfloat16))
            rights.append(jnp.concatenate(top + bottom, axis=0))

        def put(q):
            here = at // 16 + q * 16
            pick = jnp.concatenate([same & (here == to_first), same & (here == to_second)], axis=1)
            pick = pick.astype(jnp.bfloat16)
            for g, right in enumerate(rights):
                moved = jnp.dot(pick, right, preferred_element_type=jnp.float32).astype(jnp.bfloat16)
                moved = moved.reshape(16, 16, 256)
                start = r * wide + g * 16
                dense[pl.ds(q * 16, 16), start : start + 16, :] = moved[:, :, :128]
                start += nblk * wide
                dense[pl.ds(q * 16, 16), start : start + 16, :] = moved[:, :, 128:]

        if owners <= 16:
            put(0)
        else:
            pl.loop(0, owners // 16)(put)


def place_blocks(counts, cols, vals, cot, weight, bias, owners):
    nblk, slots, flat = vals.shape
    wide = flat // 128
    return pl.pallas_call(
        functools.partial(place_kernel, digit_groups(owners)),
        out_shape=(
            jax.ShapeDtypeStruct((owners, 2 * nblk * wide, 128), jnp.bfloat16),
            jax.ShapeDtypeStruct(cot.shape[::-1], cot.dtype),
            jax.ShapeDtypeStruct(weight.shape[::-1], weight.dtype),
            jax.ShapeDtypeStruct((bias.shape[1], 128), bias.dtype),
        ),
        in_specs=[SMEM] + [VMEM] * 5,
        out_specs=(VMEM,) * 4,
        compiler_params=limit(owners),
        name="place",
    )(counts, cols, vals, cot, weight, bias)


def sum_kernel(dense, *refs):
    pieces, out = refs[:-1], refs[-1]
    owners, rows, _ = dense.shape
    each = owners // len(pieces)
    acc = jnp.zeros((rows, 128), jnp.float32)
    for s, feats in enumerate(pieces):

        def two(q, acc):
            at = s * each + 2 * q
            left = jnp.concatenate([dense[at], dense[at + 1]], axis=1)
            right = feats[pl.ds(pl.multiple_of(q * 256, 256), 256), :]
            return acc + jnp.dot(left, right, preferred_element_type=jnp.float32)

        if each <= 16:
            for q in range(each // 2):
                acc = two(q, acc)
        else:
            acc = lax.fori_loop(0, each // 2, two, acc)
    nblk = rows // 64
    for p in range(2):
        for r in range(nblk):
            out[pl.ds(r * 64 + p, 32, stride=2), :] = acc[(p * nblk + r) * 32 : (p * nblk + r + 1) * 32]


def sum_blocks(dense, pieces):
    return pl.pallas_call(
        sum_kernel,
        out_shape=jax.ShapeDtypeStruct((dense.shape[1], 128), jnp.float32),
        in_specs=[VMEM] * (1 + len(pieces)),
        out_specs=VMEM,
        compiler_params=limit(dense.shape[0]),
        name="block_sum",
    )(dense, *pieces)


NT = (((1,), (1,)), ((), ()))


def layer_kernel(mine, other, weight_t, bias_t, cot_mine, cot_other, parts):
    first = lax.axis_index("rep") == 0
    owners, chunk, _ = parts.shape
    share = weight_t.shape[0] // owners
    aggregated = (mine[...] + other[...]).astype(jnp.bfloat16)
    pre = lax.dot_general(weight_t[...], aggregated, NT, preferred_element_type=jnp.float32)
    pre = pre + jnp.concatenate([bias_t[...]] * (pre.shape[1] // 128), axis=1)
    sig = 1.0 / (1.0 + jnp.exp(-pre))
    cot_a, cot_b = cot_mine[...].astype(jnp.float32), cot_other[...].astype(jnp.float32)
    cot = jnp.concatenate([jnp.where(first, cot_a, cot_b), jnp.where(first, cot_b, cot_a)], axis=1)
    delta = (cot * sig * (1.0 + pre * (1.0 - sig))).astype(jnp.bfloat16)
    grad = jnp.dot(delta, aggregated, preferred_element_type=jnp.float32)
    ones = jnp.ones((16, delta.shape[1]), jnp.bfloat16)
    total = lax.dot_general(ones, delta, NT, preferred_element_type=jnp.float32)[:1]
    blank = jnp.zeros((chunk - share - 2, 128), jnp.float32)
    tail = jnp.concatenate([total[:, :128], total[:, 128:], blank], axis=0)
    for r in range(owners):
        parts[r] = jnp.concatenate([grad[r * share : (r + 1) * share], tail], axis=0).astype(parts.dtype)


def layer(mine, other, weight_t, bias_t, cot_mine, cot_other, owners):
    share = weight_t.shape[0] // owners
    chunk = -(-(share + 2) // 16) * 16
    return pl.pallas_call(
        layer_kernel,
        out_shape=jax.ShapeDtypeStruct((owners, chunk, 128), jnp.bfloat16),
        in_specs=[VMEM] * 6,
        out_specs=VMEM,
        compiler_params=limit(owners),
        name="layer",
    )(mine, other, weight_t, bias_t, cot_mine, cot_other)


def finish_kernel(mine, other, weight, bias, got, act, weight_grad, bias_grad):
    half = act.shape[0]
    own = pl.ds(pl.multiple_of(lax.axis_index("rep") * half, half), half)
    aggregated = (mine[own, :] + other[own, :]).astype(jnp.bfloat16)
    pre = jnp.dot(aggregated, weight[...], preferred_element_type=jnp.float32) + bias[...]
    act[...] = (pre / (1.0 + jnp.exp(-pre))).astype(act.dtype)
    share = weight_grad.shape[0]
    total = jnp.sum(got[...].astype(jnp.float32), axis=0)
    weight_grad[...] = total[:share]
    flat = jnp.concatenate([total[share : share + 1], total[share + 1 : share + 2]], axis=1)
    flat = jnp.broadcast_to(flat, (8, 256))
    flat = pltpu.roll(flat, lax.rem(256 - lax.axis_index("rows") * share, 256), 1)
    bias_grad[...] = flat[:1, :share]


def finish(mine, other, weight, bias, got):
    owners = got.shape[0]
    share = weight.shape[1] // owners
    return pl.pallas_call(
        finish_kernel,
        out_shape=(
            jax.ShapeDtypeStruct((mine.shape[0] // 2, weight.shape[1]), jnp.bfloat16),
            jax.ShapeDtypeStruct((share, 128), jnp.float32),
            jax.ShapeDtypeStruct((1, share), jnp.float32),
        ),
        in_specs=[VMEM] * 5,
        out_specs=(VMEM,) * 3,
        compiler_params=limit(owners),
        name="finish",
    )(mine, other, weight, bias, got)


def body(features, weight, bias, block_count, block_cols, block_vals, cotangent):
    side = lax.axis_index("rep")
    owners = lax.axis_size("rows")
    groups = digit_groups(owners)
    half_rows = features.shape[0] // 2

    keep = lax.dynamic_slice_in_dim(features, side * half_rows, half_rows, 0)
    give = lax.dynamic_slice_in_dim(features, (1 - side) * half_rows, half_rows, 0)
    shift, radix = groups[0]
    pieces = [keep] + [across(give, s << shift, owners, 1) for s in range(1, radix)]
    vals = block_vals[0]
    for shift, radix in groups[1:]:
        held, vals = lax.optimization_barrier((jnp.concatenate(pieces), vals))
        pieces = [held] + [across(held, s << shift, owners, 0) for s in range(1, radix)]

    bias = bias.reshape(1, -1)
    dense, cot_mine, weight_t, bias_t = place_blocks(
        block_count, block_cols[0], vals, cotangent, weight, bias, owners
    )
    cot_other = across(cot_mine, 0, owners, 1)
    dense, cot_other = lax.optimization_barrier((dense, cot_other))

    mine = sum_blocks(dense, pieces)
    other = across(mine, 0, owners, 1)
    parts = layer(mine, other, weight_t, bias_t, cot_mine, cot_other, owners)
    got = lax.all_to_all(parts, "rows", split_axis=0, concat_axis=0, tiled=True)
    activated, weight_grad, bias_grad = finish(mine, other, weight, bias, got)
    return activated, weight_grad.T, bias_grad.reshape(-1)


def solution(mesh):
    placed = (
        P("rows", None),
        P(),
        P(),
        P("rep", "rows"),
        P("rep", "rows", None),
        P("rep", "rows", None, None),
        P(BOTH, None),
    )
    return jax.shard_map(
        body,
        mesh=mesh,
        in_specs=placed,
        out_specs=(P(BOTH, None), P(None, "rows"), P("rows")),
        check_vma=False,
    )
```

```python
import functools

import functools

import jax
import jax.numpy as jnp
from jax import lax
from jax.experimental import pallas as pl
from jax.experimental.pallas import tpu as pltpu
from jax.sharding import PartitionSpec as P

BOTH = ("rows", "rep")
VMEM = pl.BlockSpec(memory_space=pltpu.VMEM)
SMEM = pl.BlockSpec(memory_space=pltpu.SMEM)


def digit_groups(owners):
    top = owners.bit_length() - 1
    groups = []
    while top > 0:
        take = min(2, top)
        top -= take
        groups.append((top, 1 << take))
    return groups


def across(value, mask, owners, swap):
    pairs = [(i, i ^ (2 * mask + swap)) for i in range(2 * owners)]
    return lax.ppermute(value, BOTH, pairs)


def limit(owners):
    return pltpu.CompilerParams(vmem_limit_bytes=(8 if owners <= 16 else 48) << 20)


def place_kernel(groups, counts, cols, vals, cot, weight, bias, dense, cot_out, weight_out, bias_out):
    nblk, slots, flat = vals.shape
    owners = dense.shape[0]
    cot_out[...] = cot[...].astype(jnp.float32).T.astype(jnp.bfloat16)
    weight_out[...] = weight[...].astype(jnp.float32).T.astype(jnp.bfloat16)
    bias_out[...] = jnp.broadcast_to(bias[...], (128, bias.shape[1])).T
    wide = flat // 128
    deep = 16 * slots
    lane = lax.broadcasted_iota(jnp.int32, (slots, deep), 1)
    slot = lax.broadcasted_iota(jnp.int32, (slots, deep), 0)
    spread = (lane % slots == slot).astype(jnp.bfloat16)
    named = jnp.dot(cols[...].astype(jnp.bfloat16), spread, preferred_element_type=jnp.float32)
    named = named.astype(jnp.int32)
    apart = (named >> 1) ^ lax.axis_index("rows")
    place = jnp.zeros_like(apart)
    stride = 1
    for shift, radix in groups:
        place = place + ((apart >> shift) & (radix - 1)) * stride
        stride *= radix
    side = named & 1
    lane = lax.broadcasted_iota(jnp.int32, (1, deep), 1)
    at = lax.broadcasted_iota(jnp.int32, (256, deep), 0)
    same = at % 16 == lax.broadcasted_iota(jnp.int32, (256, deep), 1) // slots
    low = lax.broadcasted_iota(jnp.int32, (slots, 128), 1) < 64
    for r in range(nblk):
        used = lane % slots < counts[0, r]
        to_first = jnp.where(used & (side[r : r + 1] == 0), place[r : r + 1], -1)
        to_second = jnp.where(used & (side[r : r + 1] == 1), place[r : r + 1], -1)
        rights = []
        for g in range(wide // 16):
            top, bottom = [], []
            for i in range(g * 16, g * 16 + 16):
                two = vals[r, :, i * 128 : (i + 1) * 128].astype(jnp.float32)
                turned = pltpu.roll(two, 64, 1)
                top.append(jnp.concatenate([jnp.where(low, two, 0.0), jnp.where(low, turned, 0.0)], axis=1).astype(jnp.bfloat16))
                bottom.append(jnp.concatenate([jnp.where(low, 0.0, turned), jnp.where(low, 0.0, two)], axis=1).astype(jnp.bfloat16))
            rights.append(jnp.concatenate(top + bottom, axis=0))

        def put(q):
            here = at // 16 + q * 16
            pick = jnp.concatenate([same & (here == to_first), same & (here == to_second)], axis=1)
            pick = pick.astype(jnp.bfloat16)
            for g, right in enumerate(rights):
                moved = jnp.dot(pick, right, preferred_element_type=jnp.float32).astype(jnp.bfloat16)
                moved = moved.reshape(16, 16, 256)
                start = r * wide + g * 16
                dense[pl.ds(q * 16, 16), start : start + 16, :] = moved[:, :, :128]
                start += nblk * wide
                dense[pl.ds(q * 16, 16), start : start + 16, :] = moved[:, :, 128:]

        if owners <= 16:
            put(0)
        else:
            pl.loop(0, owners // 16)(put)


def place_blocks(counts, cols, vals, cot, weight, bias, owners):
    nblk, slots, flat = vals.shape
    wide = flat // 128
    return pl.pallas_call(
        functools.partial(place_kernel, digit_groups(owners)),
        out_shape=(
            jax.ShapeDtypeStruct((owners, 2 * nblk * wide, 128), jnp.bfloat16),
            jax.ShapeDtypeStruct(cot.shape[::-1], cot.dtype),
            jax.ShapeDtypeStruct(weight.shape[::-1], weight.dtype),
            jax.ShapeDtypeStruct((bias.shape[1], 128), bias.dtype),
        ),
        in_specs=[SMEM] + [VMEM] * 5,
        out_specs=(VMEM,) * 4,
        compiler_params=limit(owners),
        name="place",
    )(counts, cols, vals, cot, weight, bias)


def sum_kernel(dense, *refs):
    pieces, out = refs[:-1], refs[-1]
    owners, rows, _ = dense.shape
    each = owners // len(pieces)
    acc = jnp.zeros((rows, 128), jnp.float32)
    for s, feats in enumerate(pieces):

        def two(q, acc):
            at = s * each + 2 * q
            left = jnp.concatenate([dense[at], dense[at + 1]], axis=1)
            right = feats[pl.ds(pl.multiple_of(q * 256, 256), 256), :]
            return acc + jnp.dot(left, right, preferred_element_type=jnp.float32)

        if each <= 16:
            for q in range(each // 2):
                acc = two(q, acc)
        else:
            acc = lax.fori_loop(0, each // 2, two, acc)
    nblk = rows // 64
    for p in range(2):
        for r in range(nblk):
            out[pl.ds(r * 64 + p, 32, stride=2), :] = acc[(p * nblk + r) * 32 : (p * nblk + r + 1) * 32]


def sum_blocks(dense, pieces):
    return pl.pallas_call(
        sum_kernel,
        out_shape=jax.ShapeDtypeStruct((dense.shape[1], 128), jnp.float32),
        in_specs=[VMEM] * (1 + len(pieces)),
        out_specs=VMEM,
        compiler_params=limit(dense.shape[0]),
        name="block_sum",
    )(dense, *pieces)


NT = (((1,), (1,)), ((), ()))


def layer_kernel(mine, other, weight_t, bias_t, cot_mine, cot_other, parts):
    first = lax.axis_index("rep") == 0
    owners, chunk, _ = parts.shape
    share = weight_t.shape[0] // owners
    aggregated = (mine[...] + other[...]).astype(jnp.bfloat16)
    pre = lax.dot_general(weight_t[...], aggregated, NT, preferred_element_type=jnp.float32)
    pre = pre + jnp.concatenate([bias_t[...]] * (pre.shape[1] // 128), axis=1)
    sig = 1.0 / (1.0 + jnp.exp(-pre))
    cot_a, cot_b = cot_mine[...].astype(jnp.float32), cot_other[...].astype(jnp.float32)
    cot = jnp.concatenate([jnp.where(first, cot_a, cot_b), jnp.where(first, cot_b, cot_a)], axis=1)
    delta = (cot * sig * (1.0 + pre * (1.0 - sig))).astype(jnp.bfloat16)
    grad = jnp.dot(delta, aggregated, preferred_element_type=jnp.float32)
    ones = jnp.ones((16, delta.shape[1]), jnp.bfloat16)
    total = lax.dot_general(ones, delta, NT, preferred_element_type=jnp.float32)[:1]
    blank = jnp.zeros((chunk - share - 2, 128), jnp.float32)
    tail = jnp.concatenate([total[:, :128], total[:, 128:], blank], axis=0)
    for r in range(owners):
        parts[r] = jnp.concatenate([grad[r * share : (r + 1) * share], tail], axis=0).astype(parts.dtype)


def layer(mine, other, weight_t, bias_t, cot_mine, cot_other, owners):
    share = weight_t.shape[0] // owners
    chunk = -(-(share + 2) // 16) * 16
    return pl.pallas_call(
        layer_kernel,
        out_shape=jax.ShapeDtypeStruct((owners, chunk, 128), jnp.bfloat16),
        in_specs=[VMEM] * 6,
        out_specs=VMEM,
        compiler_params=limit(owners),
        name="layer",
    )(mine, other, weight_t, bias_t, cot_mine, cot_other)


def finish_kernel(mine, other, weight, bias, got, act, weight_grad, bias_grad):
    half = act.shape[0]
    own = pl.ds(pl.multiple_of(lax.axis_index("rep") * half, half), half)
    aggregated = (mine[own, :] + other[own, :]).astype(jnp.bfloat16)
    pre = jnp.dot(aggregated, weight[...], preferred_element_type=jnp.float32) + bias[...]
    act[...] = (pre / (1.0 + jnp.exp(-pre))).astype(act.dtype)
    share = weight_grad.shape[0]
    total = jnp.sum(got[...].astype(jnp.float32), axis=0)
    weight_grad[...] = total[:share]
    flat = jnp.concatenate([total[share : share + 1], total[share + 1 : share + 2]], axis=1)
    flat = jnp.broadcast_to(flat, (8, 256))
    flat = pltpu.roll(flat, lax.rem(256 - lax.axis_index("rows") * share, 256), 1)
    bias_grad[...] = flat[:1, :share]


def finish(mine, other, weight, bias, got):
    owners = got.shape[0]
    share = weight.shape[1] // owners
    return pl.pallas_call(
        finish_kernel,
        out_shape=(
            jax.ShapeDtypeStruct((mine.shape[0] // 2, weight.shape[1]), jnp.bfloat16),
            jax.ShapeDtypeStruct((share, 128), jnp.float32),
            jax.ShapeDtypeStruct((1, share), jnp.float32),
        ),
        in_specs=[VMEM] * 5,
        out_specs=(VMEM,) * 3,
        compiler_params=limit(owners),
        name="finish",
    )(mine, other, weight, bias, got)


def body(features, weight, bias, block_count, block_cols, block_vals, cotangent):
    side = lax.axis_index("rep")
    owners = lax.axis_size("rows")
    groups = digit_groups(owners)
    half_rows = features.shape[0] // 2

    keep = lax.dynamic_slice_in_dim(features, side * half_rows, half_rows, 0)
    shift, radix = groups[0]
    pieces = [keep] + [across(keep, s << shift, owners, 0) for s in range(1, radix)]
    vals = block_vals[0]
    for shift, radix in groups[1:]:
        held, vals = lax.optimization_barrier((jnp.concatenate(pieces), vals))
        pieces = [held] + [across(held, s << shift, owners, 0) for s in range(1, radix)]

    bias = bias.reshape(1, -1)
    dense, cot_mine, weight_t, bias_t = place_blocks(
        block_count, block_cols[0], vals, cotangent, weight, bias, owners
    )
    cot_other = across(cot_mine, 0, owners, 1)
    dense, cot_other = lax.optimization_barrier((dense, cot_other))

    mine = sum_blocks(dense, pieces)
    other = across(mine, 0, owners, 1)
    parts = layer(mine, other, weight_t, bias_t, cot_mine, cot_other, owners)
    got = lax.all_to_all(parts, "rows", split_axis=0, concat_axis=0, tiled=True)
    activated, weight_grad, bias_grad = finish(mine, other, weight, bias, got)
    return activated, weight_grad.T, bias_grad.reshape(-1)


def solution(mesh):
    placed = (
        P("rows", None),
        P(),
        P(),
        P("rep", "rows"),
        P("rep", "rows", None),
        P("rep", "rows", None, None),
        P(BOTH, None),
    )
    return jax.shard_map(
        body,
        mesh=mesh,
        in_specs=placed,
        out_specs=(P(BOTH, None), P(None, "rows"), P("rows")),
        check_vma=False,
    )
```

```python
import functools

import functools

import jax
import jax.numpy as jnp
from jax import lax
from jax.experimental import pallas as pl
from jax.experimental.pallas import tpu as pltpu
from jax.sharding import PartitionSpec as P

BOTH = ("rows", "rep")
VMEM = pl.BlockSpec(memory_space=pltpu.VMEM)
SMEM = pl.BlockSpec(memory_space=pltpu.SMEM)


def digit_groups(owners):
    top = owners.bit_length() - 1
    groups = []
    while top > 0:
        take = min(2, top)
        top -= take
        groups.append((top, 1 << take))
    return groups


def across(value, mask, owners, swap):
    pairs = [(i, i ^ (2 * mask + swap)) for i in range(2 * owners)]
    return lax.ppermute(value, BOTH, pairs)


def copy_kernel(value, out):
    out[...] = value[...]


def copies(value, count):
    out = [value]
    while len(out) < count:
        one = pl.pallas_call(
            copy_kernel,
            out_shape=jax.ShapeDtypeStruct(value.shape, value.dtype),
            in_specs=[VMEM],
            out_specs=VMEM,
            compiler_params=pltpu.CompilerParams(vmem_limit_bytes=16 << 20),
            name="copy",
        )(out[-1])
        out.append(one)
    return out


def limit(owners):
    return pltpu.CompilerParams(vmem_limit_bytes=(8 if owners <= 16 else 48) << 20)


def place_kernel(groups, counts, cols, vals, cot, weight, bias, dense, cot_out, weight_out, bias_out):
    nblk, slots, flat = vals.shape
    owners = dense.shape[0]
    cot_out[...] = cot[...].astype(jnp.float32).T.astype(jnp.bfloat16)
    weight_out[...] = weight[...].astype(jnp.float32).T.astype(jnp.bfloat16)
    bias_out[...] = jnp.broadcast_to(bias[...], (128, bias.shape[1])).T
    wide = flat // 128
    deep = 16 * slots
    lane = lax.broadcasted_iota(jnp.int32, (slots, deep), 1)
    slot = lax.broadcasted_iota(jnp.int32, (slots, deep), 0)
    spread = (lane % slots == slot).astype(jnp.bfloat16)
    named = jnp.dot(cols[...].astype(jnp.bfloat16), spread, preferred_element_type=jnp.float32)
    named = named.astype(jnp.int32)
    apart = (named >> 1) ^ lax.axis_index("rows")
    place = jnp.zeros_like(apart)
    stride = 1
    for shift, radix in groups:
        place = place + ((apart >> shift) & (radix - 1)) * stride
        stride *= radix
    side = named & 1
    lane = lax.broadcasted_iota(jnp.int32, (1, deep), 1)
    at = lax.broadcasted_iota(jnp.int32, (256, deep), 0)
    same = at % 16 == lax.broadcasted_iota(jnp.int32, (256, deep), 1) // slots
    low = lax.broadcasted_iota(jnp.int32, (slots, 128), 1) < 64
    for r in range(nblk):
        used = lane % slots < counts[0, r]
        to_first = jnp.where(used & (side[r : r + 1] == 0), place[r : r + 1], -1)
        to_second = jnp.where(used & (side[r : r + 1] == 1), place[r : r + 1], -1)
        rights = []
        for g in range(wide // 16):
            top, bottom = [], []
            for i in range(g * 16, g * 16 + 16):
                two = vals[r, :, i * 128 : (i + 1) * 128].astype(jnp.float32)
                turned = pltpu.roll(two, 64, 1)
                top.append(jnp.concatenate([jnp.where(low, two, 0.0), jnp.where(low, turned, 0.0)], axis=1).astype(jnp.bfloat16))
                bottom.append(jnp.concatenate([jnp.where(low, 0.0, turned), jnp.where(low, 0.0, two)], axis=1).astype(jnp.bfloat16))
            rights.append(jnp.concatenate(top + bottom, axis=0))

        def put(q):
            here = at // 16 + q * 16
            pick = jnp.concatenate([same & (here == to_first), same & (here == to_second)], axis=1)
            pick = pick.astype(jnp.bfloat16)
            for g, right in enumerate(rights):
                moved = jnp.dot(pick, right, preferred_element_type=jnp.float32).astype(jnp.bfloat16)
                moved = moved.reshape(16, 16, 256)
                start = r * wide + g * 16
                dense[pl.ds(q * 16, 16), start : start + 16, :] = moved[:, :, :128]
                start += nblk * wide
                dense[pl.ds(q * 16, 16), start : start + 16, :] = moved[:, :, 128:]

        if owners <= 16:
            put(0)
        else:
            pl.loop(0, owners // 16)(put)


def place_blocks(counts, cols, vals, cot, weight, bias, owners):
    nblk, slots, flat = vals.shape
    wide = flat // 128
    return pl.pallas_call(
        functools.partial(place_kernel, digit_groups(owners)),
        out_shape=(
            jax.ShapeDtypeStruct((owners, 2 * nblk * wide, 128), jnp.bfloat16),
            jax.ShapeDtypeStruct(cot.shape[::-1], cot.dtype),
            jax.ShapeDtypeStruct(weight.shape[::-1], weight.dtype),
            jax.ShapeDtypeStruct((bias.shape[1], 128), bias.dtype),
        ),
        in_specs=[SMEM] + [VMEM] * 5,
        out_specs=(VMEM,) * 4,
        compiler_params=limit(owners),
        name="place",
    )(counts, cols, vals, cot, weight, bias)


def sum_kernel(dense, *refs):
    pieces, out = refs[:-1], refs[-1]
    owners, rows, _ = dense.shape
    each = owners // len(pieces)
    acc = jnp.zeros((rows, 128), jnp.float32)
    for s, feats in enumerate(pieces):

        def two(q, acc):
            at = s * each + 2 * q
            left = jnp.concatenate([dense[at], dense[at + 1]], axis=1)
            right = feats[pl.ds(pl.multiple_of(q * 256, 256), 256), :]
            return acc + jnp.dot(left, right, preferred_element_type=jnp.float32)

        if each <= 16:
            for q in range(each // 2):
                acc = two(q, acc)
        else:
            acc = lax.fori_loop(0, each // 2, two, acc)
    nblk = rows // 64
    for p in range(2):
        for r in range(nblk):
            out[pl.ds(r * 64 + p, 32, stride=2), :] = acc[(p * nblk + r) * 32 : (p * nblk + r + 1) * 32]


def sum_blocks(dense, pieces):
    return pl.pallas_call(
        sum_kernel,
        out_shape=jax.ShapeDtypeStruct((dense.shape[1], 128), jnp.float32),
        in_specs=[VMEM] * (1 + len(pieces)),
        out_specs=VMEM,
        compiler_params=limit(dense.shape[0]),
        name="block_sum",
    )(dense, *pieces)


NT = (((1,), (1,)), ((), ()))


def layer_kernel(mine, other, weight_t, bias_t, cot_mine, cot_other, parts):
    first = lax.axis_index("rep") == 0
    owners, chunk, _ = parts.shape
    share = weight_t.shape[0] // owners
    aggregated = (mine[...] + other[...]).astype(jnp.bfloat16)
    pre = lax.dot_general(weight_t[...], aggregated, NT, preferred_element_type=jnp.float32)
    pre = pre + jnp.concatenate([bias_t[...]] * (pre.shape[1] // 128), axis=1)
    sig = 1.0 / (1.0 + jnp.exp(-pre))
    cot_a, cot_b = cot_mine[...].astype(jnp.float32), cot_other[...].astype(jnp.float32)
    cot = jnp.concatenate([jnp.where(first, cot_a, cot_b), jnp.where(first, cot_b, cot_a)], axis=1)
    delta = (cot * sig * (1.0 + pre * (1.0 - sig))).astype(jnp.bfloat16)
    grad = jnp.dot(delta, aggregated, preferred_element_type=jnp.float32)
    ones = jnp.ones((16, delta.shape[1]), jnp.bfloat16)
    total = lax.dot_general(ones, delta, NT, preferred_element_type=jnp.float32)[:1]
    blank = jnp.zeros((chunk - share - 2, 128), jnp.float32)
    tail = jnp.concatenate([total[:, :128], total[:, 128:], blank], axis=0)
    for r in range(owners):
        parts[r] = jnp.concatenate([grad[r * share : (r + 1) * share], tail], axis=0).astype(parts.dtype)


def layer(mine, other, weight_t, bias_t, cot_mine, cot_other, owners):
    share = weight_t.shape[0] // owners
    chunk = -(-(share + 2) // 16) * 16
    return pl.pallas_call(
        layer_kernel,
        out_shape=jax.ShapeDtypeStruct((owners, chunk, 128), jnp.bfloat16),
        in_specs=[VMEM] * 6,
        out_specs=VMEM,
        compiler_params=limit(owners),
        name="layer",
    )(mine, other, weight_t, bias_t, cot_mine, cot_other)


def finish_kernel(mine, other, weight, bias, got, act, weight_grad, bias_grad):
    half = act.shape[0]
    own = pl.ds(pl.multiple_of(lax.axis_index("rep") * half, half), half)
    aggregated = (mine[own, :] + other[own, :]).astype(jnp.bfloat16)
    pre = jnp.dot(aggregated, weight[...], preferred_element_type=jnp.float32) + bias[...]
    act[...] = (pre / (1.0 + jnp.exp(-pre))).astype(act.dtype)
    share = weight_grad.shape[0]
    total = jnp.sum(got[...].astype(jnp.float32), axis=0)
    weight_grad[...] = total[:share]
    flat = jnp.concatenate([total[share : share + 1], total[share + 1 : share + 2]], axis=1)
    flat = jnp.broadcast_to(flat, (8, 256))
    flat = pltpu.roll(flat, lax.rem(256 - lax.axis_index("rows") * share, 256), 1)
    bias_grad[...] = flat[:1, :share]


def finish(mine, other, weight, bias, got):
    owners = got.shape[0]
    share = weight.shape[1] // owners
    return pl.pallas_call(
        finish_kernel,
        out_shape=(
            jax.ShapeDtypeStruct((mine.shape[0] // 2, weight.shape[1]), jnp.bfloat16),
            jax.ShapeDtypeStruct((share, 128), jnp.float32),
            jax.ShapeDtypeStruct((1, share), jnp.float32),
        ),
        in_specs=[VMEM] * 5,
        out_specs=(VMEM,) * 3,
        compiler_params=limit(owners),
        name="finish",
    )(mine, other, weight, bias, got)


def body(features, weight, bias, block_count, block_cols, block_vals, cotangent):
    side = lax.axis_index("rep")
    owners = lax.axis_size("rows")
    groups = digit_groups(owners)
    half_rows = features.shape[0] // 2

    keep = lax.dynamic_slice_in_dim(features, side * half_rows, half_rows, 0)
    shift, radix = groups[0]
    sent = zip(range(1, radix), copies(keep, radix - 1))
    pieces = [keep] + [across(value, s << shift, owners, 0) for s, value in sent]
    vals = block_vals[0]
    for shift, radix in groups[1:]:
        held, vals = lax.optimization_barrier((jnp.concatenate(pieces), vals))
        sent = zip(range(1, radix), copies(held, radix - 1))
        pieces = [held] + [across(value, s << shift, owners, 0) for s, value in sent]

    bias = bias.reshape(1, -1)
    dense, cot_mine, weight_t, bias_t = place_blocks(
        block_count, block_cols[0], vals, cotangent, weight, bias, owners
    )
    cot_other = across(cot_mine, 0, owners, 1)
    dense, cot_other = lax.optimization_barrier((dense, cot_other))

    mine = sum_blocks(dense, pieces)
    other = across(mine, 0, owners, 1)
    parts = layer(mine, other, weight_t, bias_t, cot_mine, cot_other, owners)
    got = lax.all_to_all(parts, "rows", split_axis=0, concat_axis=0, tiled=True)
    activated, weight_grad, bias_grad = finish(mine, other, weight, bias, got)
    return activated, weight_grad.T, bias_grad.reshape(-1)


def solution(mesh):
    placed = (
        P("rows", None),
        P(),
        P(),
        P("rep", "rows"),
        P("rep", "rows", None),
        P("rep", "rows", None, None),
        P(BOTH, None),
    )
    return jax.shard_map(
        body,
        mesh=mesh,
        in_specs=placed,
        out_specs=(P(BOTH, None), P(None, "rows"), P("rows")),
        check_vma=False,
    )
```

```python
import functools

import functools

import jax
import jax.numpy as jnp
from jax import lax
from jax.experimental import pallas as pl
from jax.experimental.pallas import tpu as pltpu
from jax.sharding import PartitionSpec as P

BOTH = ("rows", "rep")
VMEM = pl.BlockSpec(memory_space=pltpu.VMEM)
SMEM = pl.BlockSpec(memory_space=pltpu.SMEM)


def digit_groups(owners):
    top = owners.bit_length() - 1
    groups = []
    while top > 0:
        take = min(2, top)
        top -= take
        groups.append((top, 1 << take))
    return groups


def across(value, mask, owners, swap):
    pairs = [(i, i ^ (2 * mask + swap)) for i in range(2 * owners)]
    return lax.ppermute(value, BOTH, pairs)


def copy_kernel(value, out):
    out[...] = value[...]


def copies(value, count):
    out = [value]
    while len(out) < count:
        one = pl.pallas_call(
            copy_kernel,
            out_shape=jax.ShapeDtypeStruct(value.shape, value.dtype),
            in_specs=[VMEM],
            out_specs=VMEM,
            compiler_params=pltpu.CompilerParams(vmem_limit_bytes=16 << 20),
            name="copy",
        )(out[-1])
        out.append(one)
    return out


def limit(owners):
    return pltpu.CompilerParams(vmem_limit_bytes=(8 if owners <= 16 else 48) << 20)


def place_kernel(groups, counts, cols, vals, weight, bias, dense, weight_out, bias_out):
    nblk, slots, flat = vals.shape
    owners = dense.shape[0]
    weight_out[...] = weight[...].astype(jnp.float32).T.astype(jnp.bfloat16)
    bias_out[...] = jnp.broadcast_to(bias[...], (128, bias.shape[1])).T
    wide = flat // 128
    deep = 16 * slots
    lane = lax.broadcasted_iota(jnp.int32, (slots, deep), 1)
    slot = lax.broadcasted_iota(jnp.int32, (slots, deep), 0)
    spread = (lane % slots == slot).astype(jnp.bfloat16)
    named = jnp.dot(cols[...].astype(jnp.bfloat16), spread, preferred_element_type=jnp.float32)
    named = named.astype(jnp.int32)
    apart = (named >> 1) ^ lax.axis_index("rows")
    place = jnp.zeros_like(apart)
    stride = 1
    for shift, radix in groups:
        place = place + ((apart >> shift) & (radix - 1)) * stride
        stride *= radix
    side = named & 1
    lane = lax.broadcasted_iota(jnp.int32, (1, deep), 1)
    at = lax.broadcasted_iota(jnp.int32, (256, deep), 0)
    same = at % 16 == lax.broadcasted_iota(jnp.int32, (256, deep), 1) // slots
    low = lax.broadcasted_iota(jnp.int32, (slots, 128), 1) < 64
    for r in range(nblk):
        used = lane % slots < counts[0, r]
        to_first = jnp.where(used & (side[r : r + 1] == 0), place[r : r + 1], -1)
        to_second = jnp.where(used & (side[r : r + 1] == 1), place[r : r + 1], -1)
        rights = []
        for g in range(wide // 16):
            top, bottom = [], []
            for i in range(g * 16, g * 16 + 16):
                two = vals[r, :, i * 128 : (i + 1) * 128].astype(jnp.float32)
                turned = pltpu.roll(two, 64, 1)
                top.append(jnp.concatenate([jnp.where(low, two, 0.0), jnp.where(low, turned, 0.0)], axis=1).astype(jnp.bfloat16))
                bottom.append(jnp.concatenate([jnp.where(low, 0.0, turned), jnp.where(low, 0.0, two)], axis=1).astype(jnp.bfloat16))
            rights.append(jnp.concatenate(top + bottom, axis=0))

        def put(q):
            here = at // 16 + q * 16
            pick = jnp.concatenate([same & (here == to_first), same & (here == to_second)], axis=1)
            pick = pick.astype(jnp.bfloat16)
            for g, right in enumerate(rights):
                moved = jnp.dot(pick, right, preferred_element_type=jnp.float32).astype(jnp.bfloat16)
                moved = moved.reshape(16, 16, 256)
                start = r * wide + g * 16
                dense[pl.ds(q * 16, 16), start : start + 16, :] = moved[:, :, :128]
                start += nblk * wide
                dense[pl.ds(q * 16, 16), start : start + 16, :] = moved[:, :, 128:]

        if owners <= 16:
            put(0)
        else:
            pl.loop(0, owners // 16)(put)


def place_blocks(counts, cols, vals, weight, bias, owners):
    nblk, slots, flat = vals.shape
    wide = flat // 128
    return pl.pallas_call(
        functools.partial(place_kernel, digit_groups(owners)),
        out_shape=(
            jax.ShapeDtypeStruct((owners, 2 * nblk * wide, 128), jnp.bfloat16),
            jax.ShapeDtypeStruct(weight.shape[::-1], weight.dtype),
            jax.ShapeDtypeStruct((bias.shape[1], 128), bias.dtype),
        ),
        in_specs=[SMEM] + [VMEM] * 4,
        out_specs=(VMEM,) * 3,
        compiler_params=limit(owners),
        name="place",
    )(counts, cols, vals, weight, bias)


def sum_kernel(places, last, dense, *refs):
    pieces, out = refs[:-1], refs[-1]
    rows = dense.shape[1]
    if last:
        acc, pieces = pieces[0][...], pieces[1:]
    else:
        acc = jnp.zeros((rows, 128), jnp.float32)
    for start, feats in zip(places, pieces):
        each = feats.shape[0] // 128

        def two(q, acc):
            left = jnp.concatenate([dense[start + 2 * q], dense[start + 2 * q + 1]], axis=1)
            right = feats[pl.ds(pl.multiple_of(q * 256, 256), 256), :]
            return acc + jnp.dot(left, right, preferred_element_type=jnp.float32)

        if each <= 16:
            for q in range(each // 2):
                acc = two(q, acc)
        else:
            acc = lax.fori_loop(0, each // 2, two, acc)
    if not last:
        out[...] = acc
        return
    nblk = rows // 64
    for p in range(2):
        for r in range(nblk):
            out[pl.ds(r * 64 + p, 32, stride=2), :] = acc[(p * nblk + r) * 32 : (p * nblk + r + 1) * 32]


def sum_blocks(dense, operands, places, last):
    return pl.pallas_call(
        functools.partial(sum_kernel, places, last),
        out_shape=jax.ShapeDtypeStruct((dense.shape[1], 128), jnp.float32),
        in_specs=[VMEM] * (1 + len(operands)),
        out_specs=VMEM,
        compiler_params=limit(dense.shape[0]),
        name="block_sum",
    )(dense, *operands)


def turn_kernel(mine, other, turned):
    first = lax.axis_index("rep") == 0
    half = mine.shape[0]
    here, there = mine[...].astype(jnp.float32).T, other[...].astype(jnp.float32).T
    turned[:, :half] = jnp.where(first, here, there).astype(turned.dtype)
    turned[:, half:] = jnp.where(first, there, here).astype(turned.dtype)


def turn(mine, other):
    half, wide = mine.shape
    return pl.pallas_call(
        turn_kernel,
        out_shape=jax.ShapeDtypeStruct((wide, 2 * half), mine.dtype),
        in_specs=[VMEM, VMEM],
        out_specs=VMEM,
        compiler_params=limit(16),
        name="turn",
    )(mine, other)


NT = (((1,), (1,)), ((), ()))


def layer_kernel(mine, other, weight, bias, weight_t, bias_t, cot_t, parts, act):
    owners, chunk, _ = parts.shape
    share = weight_t.shape[0] // owners
    aggregated = (mine[...] + other[...]).astype(jnp.bfloat16)
    pre = lax.dot_general(weight_t[...], aggregated, NT, preferred_element_type=jnp.float32)
    pre = pre + jnp.concatenate([bias_t[...]] * (pre.shape[1] // 128), axis=1)
    sig = 1.0 / (1.0 + jnp.exp(-pre))
    cot = cot_t[...].astype(jnp.float32)
    delta = (cot * sig * (1.0 + pre * (1.0 - sig))).astype(jnp.bfloat16)
    half = act.shape[0]
    own = pl.ds(pl.multiple_of(lax.axis_index("rep") * half, half), half)
    nodes = (mine[own, :] + other[own, :]).astype(jnp.bfloat16)
    value = jnp.dot(nodes, weight[...], preferred_element_type=jnp.float32) + bias[...]
    act[...] = (value / (1.0 + jnp.exp(-value))).astype(act.dtype)
    grad = jnp.dot(delta, aggregated, preferred_element_type=jnp.float32)
    ones = jnp.ones((16, delta.shape[1]), jnp.bfloat16)
    total = lax.dot_general(ones, delta, NT, preferred_element_type=jnp.float32)[:1]
    blank = jnp.zeros((chunk - share - 2, 128), jnp.float32)
    tail = jnp.concatenate([total[:, :128], total[:, 128:], blank], axis=0)
    for r in range(owners):
        parts[r] = jnp.concatenate([grad[r * share : (r + 1) * share], tail], axis=0).astype(parts.dtype)


def layer(mine, other, weight, bias, weight_t, bias_t, cot_t, owners):
    share = weight_t.shape[0] // owners
    chunk = -(-(share + 2) // 16) * 16
    return pl.pallas_call(
        layer_kernel,
        out_shape=(
            jax.ShapeDtypeStruct((owners, chunk, 128), jnp.bfloat16),
            jax.ShapeDtypeStruct((mine.shape[0] // 2, weight.shape[1]), jnp.bfloat16),
        ),
        in_specs=[VMEM] * 7,
        out_specs=(VMEM, VMEM),
        compiler_params=limit(owners),
        name="layer",
    )(mine, other, weight, bias, weight_t, bias_t, cot_t)


def finish_kernel(act_in, got, act, weight_grad, bias_grad):
    act[...] = act_in[...]
    share = weight_grad.shape[0]
    total = jnp.sum(got[...].astype(jnp.float32), axis=0)
    weight_grad[...] = total[:share]
    flat = jnp.concatenate([total[share : share + 1], total[share + 1 : share + 2]], axis=1)
    flat = jnp.broadcast_to(flat, (8, 256))
    flat = pltpu.roll(flat, lax.rem(256 - lax.axis_index("rows") * share, 256), 1)
    bias_grad[...] = flat[:1, :share]


def finish(act, got):
    owners = got.shape[0]
    share = act.shape[1] // owners
    return pl.pallas_call(
        finish_kernel,
        out_shape=(
            jax.ShapeDtypeStruct(act.shape, act.dtype),
            jax.ShapeDtypeStruct((share, 128), jnp.float32),
            jax.ShapeDtypeStruct((1, share), jnp.float32),
        ),
        in_specs=[VMEM] * 2,
        out_specs=(VMEM,) * 3,
        compiler_params=limit(owners),
        name="finish",
    )(act, got)


def body(features, weight, bias, block_count, block_cols, block_vals, cotangent):
    side = lax.axis_index("rep")
    owners = lax.axis_size("rows")
    groups = digit_groups(owners)
    half_rows = features.shape[0] // 2

    keep = lax.dynamic_slice_in_dim(features, side * half_rows, half_rows, 0)
    shift, radix = groups[0]
    sent = zip(range(1, radix), copies(keep, radix - 1))
    pieces = [keep] + [across(value, s << shift, owners, 0) for s, value in sent]
    vals = block_vals[0]
    for shift, radix in groups[1:]:
        held, vals, cotangent = lax.optimization_barrier((jnp.concatenate(pieces), vals, cotangent))
        sent = zip(range(1, radix), copies(held, radix - 1))
        pieces = [held] + [across(value, s << shift, owners, 0) for s, value in sent]

    bias = bias.reshape(1, -1)
    dense, weight_t, bias_t = place_blocks(block_count, block_cols[0], vals, weight, bias, owners)
    cot_t = turn(cotangent, across(cotangent, 0, owners, 1))
    dense, cot_t = lax.optimization_barrier((dense, cot_t))
    each = pieces[0].shape[0] // 128
    places = [s * each for s in range(len(pieces))]
    early = sum_blocks(dense, [pieces[s] for s in (0, len(pieces) - 1)], [places[s] for s in (0, len(pieces) - 1)], False)
    late = [s for s in range(len(pieces)) if s not in (0, len(pieces) - 1)]
    mine = sum_blocks(dense, [early] + [pieces[s] for s in late], [places[s] for s in late], True)
    other = across(mine, 0, owners, 1)
    parts, activated = layer(mine, other, weight, bias, weight_t, bias_t, cot_t, owners)
    got = lax.all_to_all(parts, "rows", split_axis=0, concat_axis=0, tiled=True)
    activated, weight_grad, bias_grad = finish(activated, got)
    return activated, weight_grad.T, bias_grad.reshape(-1)


def solution(mesh):
    placed = (
        P("rows", None),
        P(),
        P(),
        P("rep", "rows"),
        P("rep", "rows", None),
        P("rep", "rows", None, None),
        P(BOTH, None),
    )
    return jax.shard_map(
        body,
        mesh=mesh,
        in_specs=placed,
        out_specs=(P(BOTH, None), P(None, "rows"), P("rows")),
        check_vma=False,
    )
```

```python
import functools

import functools

import jax
import jax.numpy as jnp
from jax import lax
from jax.experimental import pallas as pl
from jax.experimental.pallas import tpu as pltpu
from jax.sharding import PartitionSpec as P

BOTH = ("rows", "rep")
VMEM = pl.BlockSpec(memory_space=pltpu.VMEM)
SMEM = pl.BlockSpec(memory_space=pltpu.SMEM)


def digit_groups(owners):
    top = owners.bit_length() - 1
    groups = []
    while top > 0:
        take = min(2, top)
        top -= take
        groups.append((top, 1 << take))
    return groups


def across(value, mask, owners, swap):
    pairs = [(i, i ^ (2 * mask + swap)) for i in range(2 * owners)]
    return lax.ppermute(value, BOTH, pairs)


def copy_kernel(value, out):
    out[...] = value[...]


def copies(value, count):
    out = [value]
    while len(out) < count:
        one = pl.pallas_call(
            copy_kernel,
            out_shape=jax.ShapeDtypeStruct(value.shape, value.dtype),
            in_specs=[VMEM],
            out_specs=VMEM,
            compiler_params=pltpu.CompilerParams(vmem_limit_bytes=16 << 20),
            name="copy",
        )(out[-1])
        out.append(one)
    return out


def limit(owners):
    return pltpu.CompilerParams(vmem_limit_bytes=(8 if owners <= 16 else 48) << 20)


def place_kernel(groups, counts, cols, vals, weight, bias, dense, weight_out, bias_out):
    nblk, slots, flat = vals.shape
    owners = dense.shape[0]
    weight_out[...] = weight[...].astype(jnp.float32).T.astype(jnp.bfloat16)
    bias_out[...] = jnp.broadcast_to(bias[...], (128, bias.shape[1])).T
    wide = flat // 128
    deep = 16 * slots
    lane = lax.broadcasted_iota(jnp.int32, (slots, deep), 1)
    slot = lax.broadcasted_iota(jnp.int32, (slots, deep), 0)
    spread = (lane % slots == slot).astype(jnp.bfloat16)
    named = jnp.dot(cols[...].astype(jnp.bfloat16), spread, preferred_element_type=jnp.float32)
    named = named.astype(jnp.int32)
    apart = (named >> 1) ^ lax.axis_index("rows")
    place = jnp.zeros_like(apart)
    stride = 1
    for shift, radix in groups:
        place = place + ((apart >> shift) & (radix - 1)) * stride
        stride *= radix
    side = named & 1
    lane = lax.broadcasted_iota(jnp.int32, (1, deep), 1)
    at = lax.broadcasted_iota(jnp.int32, (256, deep), 0)
    same = at % 16 == lax.broadcasted_iota(jnp.int32, (256, deep), 1) // slots
    low = lax.broadcasted_iota(jnp.int32, (slots, 128), 1) < 64
    for r in range(nblk):
        used = lane % slots < counts[0, r]
        to_first = jnp.where(used & (side[r : r + 1] == 0), place[r : r + 1], -1)
        to_second = jnp.where(used & (side[r : r + 1] == 1), place[r : r + 1], -1)
        rights = []
        for g in range(wide // 16):
            top, bottom = [], []
            for i in range(g * 16, g * 16 + 16):
                two = vals[r, :, i * 128 : (i + 1) * 128].astype(jnp.float32)
                turned = pltpu.roll(two, 64, 1)
                both = jnp.concatenate([jnp.where(low, two, 0.0), jnp.where(low, turned, 0.0)], axis=1)
                top.append(both.astype(jnp.bfloat16))
                both = jnp.concatenate([jnp.where(low, 0.0, turned), jnp.where(low, 0.0, two)], axis=1)
                bottom.append(both.astype(jnp.bfloat16))
            rights.append(jnp.concatenate(top + bottom, axis=0))

        def put(q):
            here = at // 16 + q * 16
            pick = jnp.concatenate([same & (here == to_first), same & (here == to_second)], axis=1)
            pick = pick.astype(jnp.bfloat16)
            for g, right in enumerate(rights):
                moved = jnp.dot(pick, right, preferred_element_type=jnp.float32).astype(jnp.bfloat16)
                moved = moved.reshape(16, 16, 256)
                start = r * wide + g * 16
                dense[pl.ds(q * 16, 16), start : start + 16, :] = moved[:, :, :128]
                start += nblk * wide
                dense[pl.ds(q * 16, 16), start : start + 16, :] = moved[:, :, 128:]

        if owners <= 16:
            put(0)
        else:
            pl.loop(0, owners // 16)(put)


def place_blocks(counts, cols, vals, weight, bias, owners):
    nblk, slots, flat = vals.shape
    wide = flat // 128
    return pl.pallas_call(
        functools.partial(place_kernel, digit_groups(owners)),
        out_shape=(
            jax.ShapeDtypeStruct((owners, 2 * nblk * wide, 128), jnp.bfloat16),
            jax.ShapeDtypeStruct(weight.shape[::-1], weight.dtype),
            jax.ShapeDtypeStruct((bias.shape[1], 128), bias.dtype),
        ),
        in_specs=[SMEM] + [VMEM] * 4,
        out_specs=(VMEM,) * 3,
        compiler_params=limit(owners),
        name="place",
    )(counts, cols, vals, weight, bias)


def sum_kernel(places, last, dense, *refs):
    pieces, out = refs[:-1], refs[-1]
    rows = dense.shape[1]
    if last:
        acc, pieces = pieces[0][...], pieces[1:]
    else:
        acc = jnp.zeros((rows, 128), jnp.float32)
    for start, feats in zip(places, pieces):
        each = feats.shape[0] // 128

        def two(q, acc):
            left = jnp.concatenate([dense[start + 2 * q], dense[start + 2 * q + 1]], axis=1)
            right = feats[pl.ds(pl.multiple_of(q * 256, 256), 256), :]
            return acc + jnp.dot(left, right, preferred_element_type=jnp.float32)

        if each <= 16:
            for q in range(each // 2):
                acc = two(q, acc)
        else:
            acc = lax.fori_loop(0, each // 2, two, acc)
    out[...] = acc


def sum_blocks(dense, operands, places, last):
    return pl.pallas_call(
        functools.partial(sum_kernel, places, last),
        out_shape=jax.ShapeDtypeStruct((dense.shape[1], 128), jnp.float32),
        in_specs=[VMEM] * (1 + len(operands)),
        out_specs=VMEM,
        compiler_params=limit(dense.shape[0]),
        name="block_sum",
    )(dense, *operands)


def node_at(place, nodes):
    rest = place % (nodes // 2)
    return rest // 32 * 64 + rest % 32 * 2 + place // (nodes // 2)


def turn_kernel(mine, other, turned):
    first = lax.axis_index("rep") == 0
    here, there = mine[...].astype(jnp.float32), other[...].astype(jnp.float32)
    both = jnp.concatenate([jnp.where(first, here, there), jnp.where(first, there, here)], axis=0)
    nodes = both.shape[0]
    wanted = node_at(lax.broadcasted_iota(jnp.int32, (nodes, nodes), 0), nodes)
    order = (wanted == lax.broadcasted_iota(jnp.int32, (nodes, nodes), 1)).astype(jnp.bfloat16)
    both = jnp.dot(order, both.astype(jnp.bfloat16), preferred_element_type=jnp.float32)
    turned[...] = both.T.astype(turned.dtype)


def turn(mine, other):
    half, wide = mine.shape
    return pl.pallas_call(
        turn_kernel,
        out_shape=jax.ShapeDtypeStruct((wide, 2 * half), mine.dtype),
        in_specs=[VMEM, VMEM],
        out_specs=VMEM,
        compiler_params=limit(16),
        name="turn",
    )(mine, other)


NT = (((1,), (1,)), ((), ()))


def layer_kernel(mine, other, weight, bias, weight_t, bias_t, cot_t, parts, act):
    owners, chunk, _ = parts.shape
    share = weight_t.shape[0] // owners
    aggregated = (mine[...] + other[...]).astype(jnp.bfloat16)
    pre = lax.dot_general(weight_t[...], aggregated, NT, preferred_element_type=jnp.float32)
    pre = pre + jnp.concatenate([bias_t[...]] * (pre.shape[1] // 128), axis=1)
    sig = 1.0 / (1.0 + jnp.exp(-pre))
    cot = cot_t[...].astype(jnp.float32)
    delta = (cot * sig * (1.0 + pre * (1.0 - sig))).astype(jnp.bfloat16)
    half = act.shape[0]
    own = lax.broadcasted_iota(jnp.int32, (half, 2 * half), 0) + lax.axis_index("rep") * half
    found = node_at(lax.broadcasted_iota(jnp.int32, (half, 2 * half), 1), 2 * half)
    nodes = jnp.dot((found == own).astype(jnp.bfloat16), aggregated, preferred_element_type=jnp.float32)
    value = jnp.dot(nodes.astype(jnp.bfloat16), weight[...], preferred_element_type=jnp.float32) + bias[...]
    act[...] = (value / (1.0 + jnp.exp(-value))).astype(act.dtype)
    grad = jnp.dot(delta, aggregated, preferred_element_type=jnp.float32)
    ones = jnp.ones((16, delta.shape[1]), jnp.bfloat16)
    total = lax.dot_general(ones, delta, NT, preferred_element_type=jnp.float32)[:1]
    blank = jnp.zeros((chunk - share - 2, 128), jnp.float32)
    tail = jnp.concatenate([total[:, :128], total[:, 128:], blank], axis=0)
    for r in range(owners):
        parts[r] = jnp.concatenate([grad[r * share : (r + 1) * share], tail], axis=0).astype(parts.dtype)


def layer(mine, other, weight, bias, weight_t, bias_t, cot_t, owners):
    share = weight_t.shape[0] // owners
    chunk = -(-(share + 2) // 16) * 16
    return pl.pallas_call(
        layer_kernel,
        out_shape=(
            jax.ShapeDtypeStruct((owners, chunk, 128), jnp.bfloat16),
            jax.ShapeDtypeStruct((mine.shape[0] // 2, weight.shape[1]), jnp.bfloat16),
        ),
        in_specs=[VMEM] * 7,
        out_specs=(VMEM, VMEM),
        compiler_params=limit(owners),
        name="layer",
    )(mine, other, weight, bias, weight_t, bias_t, cot_t)


def finish_kernel(act_in, got, act, weight_grad, bias_grad):
    act[...] = act_in[...]
    share = weight_grad.shape[0]
    total = jnp.sum(got[...].astype(jnp.float32), axis=0)
    weight_grad[...] = total[:share]
    flat = jnp.concatenate([total[share : share + 1], total[share + 1 : share + 2]], axis=1)
    flat = jnp.broadcast_to(flat, (8, 256))
    flat = pltpu.roll(flat, lax.rem(256 - lax.axis_index("rows") * share, 256), 1)
    bias_grad[...] = flat[:1, :share]


def finish(act, got):
    owners = got.shape[0]
    share = act.shape[1] // owners
    return pl.pallas_call(
        finish_kernel,
        out_shape=(
            jax.ShapeDtypeStruct(act.shape, act.dtype),
            jax.ShapeDtypeStruct((share, 128), jnp.float32),
            jax.ShapeDtypeStruct((1, share), jnp.float32),
        ),
        in_specs=[VMEM] * 2,
        out_specs=(VMEM,) * 3,
        compiler_params=limit(owners),
        name="finish",
    )(act, got)


def body(features, weight, bias, block_count, block_cols, block_vals, cotangent):
    side = lax.axis_index("rep")
    owners = lax.axis_size("rows")
    groups = digit_groups(owners)
    half_rows = features.shape[0] // 2

    keep = lax.dynamic_slice_in_dim(features, side * half_rows, half_rows, 0)
    shift, radix = groups[0]
    sent = zip(range(1, radix), copies(keep, radix - 1))
    pieces = [keep] + [across(value, s << shift, owners, 0) for s, value in sent]
    vals = block_vals[0]
    for shift, radix in groups[1:]:
        held, vals, cotangent = lax.optimization_barrier((jnp.concatenate(pieces), vals, cotangent))
        sent = zip(range(1, radix), copies(held, radix - 1))
        pieces = [held] + [across(value, s << shift, owners, 0) for s, value in sent]

    bias = bias.reshape(1, -1)
    dense, weight_t, bias_t = place_blocks(block_count, block_cols[0], vals, weight, bias, owners)
    cot_t = turn(cotangent, across(cotangent, 0, owners, 1))
    dense, cot_t = lax.optimization_barrier((dense, cot_t))
    each = pieces[0].shape[0] // 128
    places = [s * each for s in range(len(pieces))]
    ends = (0, len(pieces) - 1)
    early = sum_blocks(dense, [pieces[s] for s in ends], [places[s] for s in ends], False)
    late = [s for s in range(len(pieces)) if s not in ends]
    mine = sum_blocks(dense, [early] + [pieces[s] for s in late], [places[s] for s in late], True)
    other = across(mine, 0, owners, 1)
    parts, activated = layer(mine, other, weight, bias, weight_t, bias_t, cot_t, owners)
    got = lax.all_to_all(parts, "rows", split_axis=0, concat_axis=0, tiled=True)
    activated, weight_grad, bias_grad = finish(activated, got)
    return activated, weight_grad.T, bias_grad.reshape(-1)


def solution(mesh):
    placed = (
        P("rows", None),
        P(),
        P(),
        P("rep", "rows"),
        P("rep", "rows", None),
        P("rep", "rows", None, None),
        P(BOTH, None),
    )
    return jax.shard_map(
        body,
        mesh=mesh,
        in_specs=placed,
        out_specs=(P(BOTH, None), P(None, "rows"), P("rows")),
        check_vma=False,
    )
```

```python
import functools

import functools

import jax
import jax.numpy as jnp
from jax import lax
from jax.experimental import pallas as pl
from jax.experimental.pallas import tpu as pltpu
from jax.sharding import PartitionSpec as P

BOTH = ("rows", "rep")
VMEM = pl.BlockSpec(memory_space=pltpu.VMEM)
SMEM = pl.BlockSpec(memory_space=pltpu.SMEM)


def digit_groups(owners):
    top = owners.bit_length() - 1
    groups = []
    while top > 0:
        take = min(2, top)
        top -= take
        groups.append((top, 1 << take))
    return groups


def across(value, mask, owners, swap):
    pairs = [(i, i ^ (2 * mask + swap)) for i in range(2 * owners)]
    return lax.ppermute(value, BOTH, pairs)


def copy_kernel(value, out):
    out[...] = value[...]


def copies(value, count):
    out = [value]
    while len(out) < count:
        one = pl.pallas_call(
            copy_kernel,
            out_shape=jax.ShapeDtypeStruct(value.shape, value.dtype),
            in_specs=[VMEM],
            out_specs=VMEM,
            compiler_params=pltpu.CompilerParams(vmem_limit_bytes=16 << 20),
            name="copy",
        )(out[-1])
        out.append(one)
    return out


def limit(owners):
    return pltpu.CompilerParams(vmem_limit_bytes=(8 if owners <= 16 else 48) << 20)


def place_kernel(groups, counts, cols, vals, weight, bias, dense, weight_out, bias_out):
    nblk, slots, flat = vals.shape
    owners = dense.shape[0]
    weight_out[...] = weight[...].astype(jnp.float32).T.astype(jnp.bfloat16)
    bias_out[...] = jnp.broadcast_to(bias[...], (128, bias.shape[1])).T
    wide = flat // 128
    deep = 16 * slots
    lane = lax.broadcasted_iota(jnp.int32, (slots, deep), 1)
    slot = lax.broadcasted_iota(jnp.int32, (slots, deep), 0)
    spread = (lane % slots == slot).astype(jnp.bfloat16)
    named = jnp.dot(cols[...].astype(jnp.bfloat16), spread, preferred_element_type=jnp.float32)
    named = named.astype(jnp.int32)
    apart = (named >> 1) ^ lax.axis_index("rows")
    place = jnp.zeros_like(apart)
    stride = 1
    for shift, radix in groups:
        place = place + ((apart >> shift) & (radix - 1)) * stride
        stride *= radix
    side = named & 1
    lane = lax.broadcasted_iota(jnp.int32, (1, deep), 1)
    at = lax.broadcasted_iota(jnp.int32, (256, deep), 0)
    same = at % 16 == lax.broadcasted_iota(jnp.int32, (256, deep), 1) // slots
    low = lax.broadcasted_iota(jnp.int32, (slots, 128), 1) < 64
    for r in range(nblk):
        used = lane % slots < counts[0, r]
        to_first = jnp.where(used & (side[r : r + 1] == 0), place[r : r + 1], -1)
        to_second = jnp.where(used & (side[r : r + 1] == 1), place[r : r + 1], -1)
        rights = []
        for g in range(wide // 16):
            top, bottom = [], []
            for i in range(g * 16, g * 16 + 16):
                two = vals[r, :, i * 128 : (i + 1) * 128].astype(jnp.float32)
                turned = pltpu.roll(two, 64, 1)
                both = jnp.concatenate([jnp.where(low, two, 0.0), jnp.where(low, turned, 0.0)], axis=1)
                top.append(both.astype(jnp.bfloat16))
                both = jnp.concatenate([jnp.where(low, 0.0, turned), jnp.where(low, 0.0, two)], axis=1)
                bottom.append(both.astype(jnp.bfloat16))
            rights.append(jnp.concatenate(top + bottom, axis=0))

        def put(q):
            here = at // 16 + q * 16
            pick = jnp.concatenate([same & (here == to_first), same & (here == to_second)], axis=1)
            pick = pick.astype(jnp.bfloat16)
            for g, right in enumerate(rights):
                moved = jnp.dot(pick, right, preferred_element_type=jnp.float32).astype(jnp.bfloat16)
                moved = moved.reshape(16, 16, 256)
                start = r * wide + g * 16
                dense[pl.ds(q * 16, 16), start : start + 16, :] = moved[:, :, :128]
                start += nblk * wide
                dense[pl.ds(q * 16, 16), start : start + 16, :] = moved[:, :, 128:]

        if owners <= 16:
            put(0)
        else:
            pl.loop(0, owners // 16)(put)


def place_blocks(counts, cols, vals, weight, bias, owners):
    nblk, slots, flat = vals.shape
    wide = flat // 128
    return pl.pallas_call(
        functools.partial(place_kernel, digit_groups(owners)),
        out_shape=(
            jax.ShapeDtypeStruct((owners, 2 * nblk * wide, 128), jnp.bfloat16),
            jax.ShapeDtypeStruct(weight.shape[::-1], weight.dtype),
            jax.ShapeDtypeStruct((bias.shape[1], 128), bias.dtype),
        ),
        in_specs=[SMEM] + [VMEM] * 4,
        out_specs=(VMEM,) * 3,
        compiler_params=limit(owners),
        name="place",
    )(counts, cols, vals, weight, bias)


def sum_kernel(places, last, dense, *refs):
    pieces, out = refs[:-1], refs[-1]
    rows = dense.shape[1]
    if last:
        acc, pieces = pieces[0][...], pieces[1:]
    else:
        acc = jnp.zeros((rows, 128), jnp.float32)
    for start, feats in zip(places, pieces):
        each = feats.shape[0] // 128

        def two(q, acc):
            left = jnp.concatenate([dense[start + 2 * q], dense[start + 2 * q + 1]], axis=1)
            right = feats[pl.ds(pl.multiple_of(q * 256, 256), 256), :]
            return acc + jnp.dot(left, right, preferred_element_type=jnp.float32)

        if each <= 16:
            for q in range(each // 2):
                acc = two(q, acc)
        else:
            acc = lax.fori_loop(0, each // 2, two, acc)
    out[...] = acc


def sum_blocks(dense, operands, places, last):
    return pl.pallas_call(
        functools.partial(sum_kernel, places, last),
        out_shape=jax.ShapeDtypeStruct((dense.shape[1], 128), jnp.float32),
        in_specs=[VMEM] * (1 + len(operands)),
        out_specs=VMEM,
        compiler_params=limit(dense.shape[0]),
        name="block_sum",
    )(dense, *operands)


def node_at(place, nodes):
    rest = place % (nodes // 2)
    return rest // 32 * 64 + rest % 32 * 2 + place // (nodes // 2)


def turn_kernel(mine, other, turned):
    first = lax.axis_index("rep") == 0
    here, there = mine[...].astype(jnp.float32), other[...].astype(jnp.float32)
    both = jnp.concatenate([jnp.where(first, here, there), jnp.where(first, there, here)], axis=0)
    nodes = both.shape[0]
    wanted = node_at(lax.broadcasted_iota(jnp.int32, (nodes, nodes), 0), nodes)
    order = (wanted == lax.broadcasted_iota(jnp.int32, (nodes, nodes), 1)).astype(jnp.bfloat16)
    both = jnp.dot(order, both.astype(jnp.bfloat16), preferred_element_type=jnp.float32)
    turned[...] = both.T.astype(turned.dtype)


def turn(mine, other):
    half, wide = mine.shape
    return pl.pallas_call(
        turn_kernel,
        out_shape=jax.ShapeDtypeStruct((wide, 2 * half), mine.dtype),
        in_specs=[VMEM, VMEM],
        out_specs=VMEM,
        compiler_params=limit(16),
        name="turn",
    )(mine, other)


NT = (((1,), (1,)), ((), ()))


def layer_kernel(mine, other, weight, bias, weight_t, bias_t, cot_t, parts, act):
    owners, chunk, _ = parts.shape
    share = weight_t.shape[0] // owners
    aggregated = (mine[...] + other[...]).astype(jnp.bfloat16)
    pre = lax.dot_general(weight_t[...], aggregated, NT, preferred_element_type=jnp.float32)
    pre = pre + jnp.concatenate([bias_t[...]] * (pre.shape[1] // 128), axis=1)
    sig = 1.0 / (1.0 + jnp.exp(-pre))
    cot = cot_t[...].astype(jnp.float32)
    delta = (cot * sig * (1.0 + pre * (1.0 - sig))).astype(jnp.bfloat16)
    half = act.shape[0]
    own = lax.broadcasted_iota(jnp.int32, (half, 2 * half), 0) + lax.axis_index("rep") * half
    found = node_at(lax.broadcasted_iota(jnp.int32, (half, 2 * half), 1), 2 * half)
    nodes = jnp.dot((found == own).astype(jnp.bfloat16), aggregated, preferred_element_type=jnp.float32)
    value = jnp.dot(nodes.astype(jnp.bfloat16), weight[...], preferred_element_type=jnp.float32) + bias[...]
    act[...] = (value / (1.0 + jnp.exp(-value))).astype(act.dtype)
    grad = jnp.dot(delta, aggregated, preferred_element_type=jnp.float32)
    ones = jnp.ones((16, delta.shape[1]), jnp.bfloat16)
    total = lax.dot_general(ones, delta, NT, preferred_element_type=jnp.float32)[:1]
    blank = jnp.zeros((chunk - share - 2, 128), jnp.float32)
    tail = jnp.concatenate([total[:, :128], total[:, 128:], blank], axis=0)
    for r in range(owners):
        parts[r] = jnp.concatenate([grad[r * share : (r + 1) * share], tail], axis=0).astype(parts.dtype)


def layer(mine, other, weight, bias, weight_t, bias_t, cot_t, owners):
    share = weight_t.shape[0] // owners
    chunk = -(-(share + 2) // 16) * 16
    return pl.pallas_call(
        layer_kernel,
        out_shape=(
            jax.ShapeDtypeStruct((owners, chunk, 128), jnp.bfloat16),
            jax.ShapeDtypeStruct((mine.shape[0] // 2, weight.shape[1]), jnp.bfloat16),
        ),
        in_specs=[VMEM] * 7,
        out_specs=(VMEM, VMEM),
        compiler_params=limit(owners),
        name="layer",
    )(mine, other, weight, bias, weight_t, bias_t, cot_t)


def finish_kernel(act_in, got, act, weight_grad, bias_grad, sem):
    copy = pltpu.make_async_copy(act_in, act, sem)
    copy.start()
    share = weight_grad.shape[0]
    total = jnp.sum(got[...].astype(jnp.float32), axis=0)
    weight_grad[...] = total[:share]
    flat = jnp.concatenate([total[share : share + 1], total[share + 1 : share + 2]], axis=1)
    flat = jnp.broadcast_to(flat, (8, 256))
    flat = pltpu.roll(flat, lax.rem(256 - lax.axis_index("rows") * share, 256), 1)
    bias_grad[...] = flat[:1, :share]
    copy.wait()


def finish(act, got):
    owners = got.shape[0]
    share = act.shape[1] // owners
    return pl.pallas_call(
        finish_kernel,
        out_shape=(
            jax.ShapeDtypeStruct(act.shape, act.dtype),
            jax.ShapeDtypeStruct((share, 128), jnp.float32),
            jax.ShapeDtypeStruct((1, share), jnp.float32),
        ),
        in_specs=[VMEM] * 2,
        out_specs=(pl.BlockSpec(memory_space=pltpu.HBM), VMEM, VMEM),
        scratch_shapes=[pltpu.SemaphoreType.DMA],
        compiler_params=limit(owners),
        name="finish",
    )(act, got)


def body(features, weight, bias, block_count, block_cols, block_vals, cotangent):
    side = lax.axis_index("rep")
    owners = lax.axis_size("rows")
    groups = digit_groups(owners)
    half_rows = features.shape[0] // 2

    keep = lax.dynamic_slice_in_dim(features, side * half_rows, half_rows, 0)
    shift, radix = groups[0]
    sent = zip(range(1, radix), copies(keep, radix - 1))
    pieces = [keep] + [across(value, s << shift, owners, 0) for s, value in sent]
    vals = block_vals[0]
    for shift, radix in groups[1:]:
        held, vals, cotangent = lax.optimization_barrier((jnp.concatenate(pieces), vals, cotangent))
        sent = zip(range(1, radix), copies(held, radix - 1))
        pieces = [held] + [across(value, s << shift, owners, 0) for s, value in sent]

    bias = bias.reshape(1, -1)
    dense, weight_t, bias_t = place_blocks(block_count, block_cols[0], vals, weight, bias, owners)
    cot_t = turn(cotangent, across(cotangent, 0, owners, 1))
    dense, cot_t = lax.optimization_barrier((dense, cot_t))
    each = pieces[0].shape[0] // 128
    places = [s * each for s in range(len(pieces))]
    ends = (0, len(pieces) - 1)
    early = sum_blocks(dense, [pieces[s] for s in ends], [places[s] for s in ends], False)
    late = [s for s in range(len(pieces)) if s not in ends]
    mine = sum_blocks(dense, [early] + [pieces[s] for s in late], [places[s] for s in late], True)
    other = across(mine, 0, owners, 1)
    parts, activated = layer(mine, other, weight, bias, weight_t, bias_t, cot_t, owners)
    got = lax.all_to_all(parts, "rows", split_axis=0, concat_axis=0, tiled=True)
    activated, weight_grad, bias_grad = finish(activated, got)
    return activated, weight_grad.T, bias_grad.reshape(-1)


def solution(mesh):
    placed = (
        P("rows", None),
        P(),
        P(),
        P("rep", "rows"),
        P("rep", "rows", None),
        P("rep", "rows", None, None),
        P(BOTH, None),
    )
    return jax.shard_map(
        body,
        mesh=mesh,
        in_specs=placed,
        out_specs=(P(BOTH, None), P(None, "rows"), P("rows")),
        check_vma=False,
    )
```

```python
import functools

import functools

import jax
import jax.numpy as jnp
from jax import lax
from jax.experimental import pallas as pl
from jax.experimental.pallas import tpu as pltpu
from jax.sharding import PartitionSpec as P

BOTH = ("rows", "rep")
VMEM = pl.BlockSpec(memory_space=pltpu.VMEM)
SMEM = pl.BlockSpec(memory_space=pltpu.SMEM)


def digit_groups(owners):
    top = owners.bit_length() - 1
    groups = []
    while top > 0:
        take = min(2, top)
        top -= take
        groups.append((top, 1 << take))
    return groups


def across(value, mask, owners, swap):
    pairs = [(i, i ^ (2 * mask + swap)) for i in range(2 * owners)]
    return lax.ppermute(value, BOTH, pairs)


def copy_kernel(value, out):
    out[...] = value[...]


def copies(value, count):
    out = [value]
    while len(out) < count:
        one = pl.pallas_call(
            copy_kernel,
            out_shape=jax.ShapeDtypeStruct(value.shape, value.dtype),
            in_specs=[VMEM],
            out_specs=VMEM,
            compiler_params=pltpu.CompilerParams(vmem_limit_bytes=16 << 20),
            name="copy",
        )(out[-1])
        out.append(one)
    return out


def limit(owners):
    return pltpu.CompilerParams(vmem_limit_bytes=(8 if owners <= 16 else 48) << 20)


def place_kernel(groups, counts, cols, vals, weight, bias, dense, weight_out, bias_out):
    nblk, slots, flat = vals.shape
    owners = dense.shape[0]
    weight_out[...] = weight[...].astype(jnp.float32).T.astype(jnp.bfloat16)
    bias_out[...] = jnp.broadcast_to(bias[...], (128, bias.shape[1])).T
    wide = flat // 128
    deep = 16 * slots
    lane = lax.broadcasted_iota(jnp.int32, (slots, deep), 1)
    slot = lax.broadcasted_iota(jnp.int32, (slots, deep), 0)
    spread = (lane % slots == slot).astype(jnp.bfloat16)
    named = jnp.dot(cols[...].astype(jnp.bfloat16), spread, preferred_element_type=jnp.float32)
    named = named.astype(jnp.int32)
    apart = (named >> 1) ^ lax.axis_index("rows")
    place = jnp.zeros_like(apart)
    stride = 1
    for shift, radix in groups:
        place = place + ((apart >> shift) & (radix - 1)) * stride
        stride *= radix
    side = named & 1
    lane = lax.broadcasted_iota(jnp.int32, (1, deep), 1)
    at = lax.broadcasted_iota(jnp.int32, (256, deep), 0)
    same = at % 16 == lax.broadcasted_iota(jnp.int32, (256, deep), 1) // slots
    low = lax.broadcasted_iota(jnp.int32, (slots, 128), 1) < 64
    for r in range(nblk):
        used = lane % slots < counts[0, r]
        to_first = jnp.where(used & (side[r : r + 1] == 0), place[r : r + 1], -1)
        to_second = jnp.where(used & (side[r : r + 1] == 1), place[r : r + 1], -1)
        rights = []
        for g in range(wide // 16):
            top, bottom = [], []
            for i in range(g * 16, g * 16 + 16):
                two = vals[r, :, i * 128 : (i + 1) * 128].astype(jnp.float32)
                turned = pltpu.roll(two, 64, 1)
                both = jnp.concatenate([jnp.where(low, two, 0.0), jnp.where(low, turned, 0.0)], axis=1)
                top.append(both.astype(jnp.bfloat16))
                both = jnp.concatenate([jnp.where(low, 0.0, turned), jnp.where(low, 0.0, two)], axis=1)
                bottom.append(both.astype(jnp.bfloat16))
            rights.append(jnp.concatenate(top + bottom, axis=0))

        def put(q):
            here = at // 16 + q * 16
            pick = jnp.concatenate([same & (here == to_first), same & (here == to_second)], axis=1)
            pick = pick.astype(jnp.bfloat16)
            for g, right in enumerate(rights):
                moved = jnp.dot(pick, right, preferred_element_type=jnp.float32).astype(jnp.bfloat16)
                moved = moved.reshape(16, 16, 256)
                start = r * wide + g * 16
                dense[pl.ds(q * 16, 16), start : start + 16, :] = moved[:, :, :128]
                start += nblk * wide
                dense[pl.ds(q * 16, 16), start : start + 16, :] = moved[:, :, 128:]

        if owners <= 16:
            put(0)
        else:
            pl.loop(0, owners // 16)(put)


def place_blocks(counts, cols, vals, weight, bias, owners):
    nblk, slots, flat = vals.shape
    wide = flat // 128
    return pl.pallas_call(
        functools.partial(place_kernel, digit_groups(owners)),
        out_shape=(
            jax.ShapeDtypeStruct((owners, 2 * nblk * wide, 128), jnp.bfloat16),
            jax.ShapeDtypeStruct(weight.shape[::-1], weight.dtype),
            jax.ShapeDtypeStruct((bias.shape[1], 128), bias.dtype),
        ),
        in_specs=[SMEM] + [VMEM] * 4,
        out_specs=(VMEM,) * 3,
        compiler_params=limit(owners),
        name="place",
    )(counts, cols, vals, weight, bias)


def sum_kernel(places, last, dense, *refs):
    pieces, out = refs[:-1], refs[-1]
    rows = dense.shape[1]
    if last:
        acc, pieces = pieces[0][...], pieces[1:]
    else:
        acc = jnp.zeros((rows, 128), jnp.float32)
    for start, feats in zip(places, pieces):
        each = feats.shape[0] // 128

        def two(q, acc):
            left = jnp.concatenate([dense[start + 2 * q], dense[start + 2 * q + 1]], axis=1)
            right = feats[pl.ds(pl.multiple_of(q * 256, 256), 256), :]
            return acc + jnp.dot(left, right, preferred_element_type=jnp.float32)

        if each <= 16:
            for q in range(each // 2):
                acc = two(q, acc)
        else:
            acc = lax.fori_loop(0, each // 2, two, acc)
    out[...] = acc


def sum_blocks(dense, operands, places, last):
    return pl.pallas_call(
        functools.partial(sum_kernel, places, last),
        out_shape=jax.ShapeDtypeStruct((dense.shape[1], 128), jnp.float32),
        in_specs=[VMEM] * (1 + len(operands)),
        out_specs=VMEM,
        compiler_params=limit(dense.shape[0]),
        name="block_sum",
    )(dense, *operands)


def node_at(place, nodes):
    rest = place % (nodes // 2)
    return rest // 32 * 64 + rest % 32 * 2 + place // (nodes // 2)


def turn_kernel(mine, other, turned):
    first = lax.axis_index("rep") == 0
    here, there = mine[...].astype(jnp.float32), other[...].astype(jnp.float32)
    both = jnp.concatenate([jnp.where(first, here, there), jnp.where(first, there, here)], axis=0)
    nodes = both.shape[0]
    wanted = node_at(lax.broadcasted_iota(jnp.int32, (nodes, nodes), 0), nodes)
    order = (wanted == lax.broadcasted_iota(jnp.int32, (nodes, nodes), 1)).astype(jnp.bfloat16)
    both = jnp.dot(order, both.astype(jnp.bfloat16), preferred_element_type=jnp.float32)
    turned[...] = both.T.astype(turned.dtype)


def turn(mine, other):
    half, wide = mine.shape
    return pl.pallas_call(
        turn_kernel,
        out_shape=jax.ShapeDtypeStruct((wide, 2 * half), mine.dtype),
        in_specs=[VMEM, VMEM],
        out_specs=VMEM,
        compiler_params=limit(16),
        name="turn",
    )(mine, other)


NT = (((1,), (1,)), ((), ()))


def layer_kernel(mine, other, weight, bias, weight_t, bias_t, cot_t, parts, act):
    owners, chunk, _ = parts.shape
    share = weight_t.shape[0] // owners
    aggregated = (mine[...] + other[...]).astype(jnp.bfloat16)
    pre = lax.dot_general(weight_t[...], aggregated, NT, preferred_element_type=jnp.float32)
    pre = pre + jnp.concatenate([bias_t[...]] * (pre.shape[1] // 128), axis=1)
    sig = 1.0 / (1.0 + jnp.exp(-pre))
    cot = cot_t[...].astype(jnp.float32)
    delta = (cot * sig * (1.0 + pre * (1.0 - sig))).astype(jnp.bfloat16)
    half = act.shape[0]
    own = lax.broadcasted_iota(jnp.int32, (half, 2 * half), 0) + lax.axis_index("rep") * half
    found = node_at(lax.broadcasted_iota(jnp.int32, (half, 2 * half), 1), 2 * half)
    nodes = jnp.dot((found == own).astype(jnp.bfloat16), aggregated, preferred_element_type=jnp.float32)
    value = jnp.dot(nodes.astype(jnp.bfloat16), weight[...], preferred_element_type=jnp.float32) + bias[...]
    act[...] = (value / (1.0 + jnp.exp(-value))).astype(act.dtype)
    grad = jnp.dot(delta, aggregated, preferred_element_type=jnp.float32)
    ones = jnp.ones((16, delta.shape[1]), jnp.bfloat16)
    total = lax.dot_general(ones, delta, NT, preferred_element_type=jnp.float32)[:1]
    blank = jnp.zeros((chunk - share - 2, 128), jnp.float32)
    tail = jnp.concatenate([total[:, :128], total[:, 128:], blank], axis=0)
    for r in range(owners):
        parts[r] = jnp.concatenate([grad[r * share : (r + 1) * share], tail], axis=0).astype(parts.dtype)


def layer(mine, other, weight, bias, weight_t, bias_t, cot_t, owners):
    share = weight_t.shape[0] // owners
    chunk = -(-(share + 2) // 16) * 16
    return pl.pallas_call(
        layer_kernel,
        out_shape=(
            jax.ShapeDtypeStruct((owners, chunk, 128), jnp.bfloat16),
            jax.ShapeDtypeStruct((mine.shape[0] // 2, weight.shape[1]), jnp.bfloat16),
        ),
        in_specs=[VMEM] * 7,
        out_specs=(VMEM, VMEM),
        compiler_params=limit(owners),
        name="layer",
    )(mine, other, weight, bias, weight_t, bias_t, cot_t)


def finish_kernel(act_in, got, act, weight_out, bias_out, weight_grad, bias_grad, sems):
    pairs = ((act_in, act), (weight_grad, weight_out), (bias_grad, bias_out))
    copies_out = [pltpu.make_async_copy(a, b, sems.at[i]) for i, (a, b) in enumerate(pairs)]
    copies_out[0].start()
    share = weight_grad.shape[0]
    total = jnp.sum(got[...].astype(jnp.float32), axis=0)
    weight_grad[...] = total[:share]
    copies_out[1].start()
    flat = jnp.concatenate([total[share : share + 1], total[share + 1 : share + 2]], axis=1)
    flat = jnp.broadcast_to(flat, (8, 256))
    flat = pltpu.roll(flat, lax.rem(256 - lax.axis_index("rows") * share, 256), 1)
    bias_grad[...] = flat[:1, :share]
    copies_out[2].start()
    for copy in copies_out:
        copy.wait()


def finish(act, got):
    owners = got.shape[0]
    share = act.shape[1] // owners
    return pl.pallas_call(
        finish_kernel,
        out_shape=(
            jax.ShapeDtypeStruct(act.shape, act.dtype),
            jax.ShapeDtypeStruct((share, 128), jnp.float32),
            jax.ShapeDtypeStruct((1, share), jnp.float32),
        ),
        in_specs=[VMEM] * 2,
        out_specs=(pl.BlockSpec(memory_space=pltpu.HBM),) * 3,
        scratch_shapes=[
            pltpu.VMEM((share, 128), jnp.float32),
            pltpu.VMEM((1, share), jnp.float32),
            pltpu.SemaphoreType.DMA((3,)),
        ],
        compiler_params=limit(owners),
        name="finish",
    )(act, got)


def body(features, weight, bias, block_count, block_cols, block_vals, cotangent):
    side = lax.axis_index("rep")
    owners = lax.axis_size("rows")
    groups = digit_groups(owners)
    half_rows = features.shape[0] // 2

    keep = lax.dynamic_slice_in_dim(features, side * half_rows, half_rows, 0)
    shift, radix = groups[0]
    sent = zip(range(1, radix), copies(keep, radix - 1))
    pieces = [keep] + [across(value, s << shift, owners, 0) for s, value in sent]
    vals = block_vals[0]
    for shift, radix in groups[1:]:
        held, vals, cotangent = lax.optimization_barrier((jnp.concatenate(pieces), vals, cotangent))
        sent = zip(range(1, radix), copies(held, radix - 1))
        pieces = [held] + [across(value, s << shift, owners, 0) for s, value in sent]

    bias = bias.reshape(1, -1)
    dense, weight_t, bias_t = place_blocks(block_count, block_cols[0], vals, weight, bias, owners)
    cot_t = turn(cotangent, across(cotangent, 0, owners, 1))
    dense, cot_t = lax.optimization_barrier((dense, cot_t))
    each = pieces[0].shape[0] // 128
    places = [s * each for s in range(len(pieces))]
    ends = (0, len(pieces) - 1)
    early = sum_blocks(dense, [pieces[s] for s in ends], [places[s] for s in ends], False)
    late = [s for s in range(len(pieces)) if s not in ends]
    mine = sum_blocks(dense, [early] + [pieces[s] for s in late], [places[s] for s in late], True)
    other = across(mine, 0, owners, 1)
    parts, activated = layer(mine, other, weight, bias, weight_t, bias_t, cot_t, owners)
    got = lax.all_to_all(parts, "rows", split_axis=0, concat_axis=0, tiled=True)
    activated, weight_grad, bias_grad = finish(activated, got)
    return activated, weight_grad.T, bias_grad.reshape(-1)


def solution(mesh):
    placed = (
        P("rows", None),
        P(),
        P(),
        P("rep", "rows"),
        P("rep", "rows", None),
        P("rep", "rows", None, None),
        P(BOTH, None),
    )
    return jax.shard_map(
        body,
        mesh=mesh,
        in_specs=placed,
        out_specs=(P(BOTH, None), P(None, "rows"), P("rows")),
        check_vma=False,
    )
```

```python
import functools

import functools

import jax
import jax.numpy as jnp
from jax import lax
from jax.experimental import pallas as pl
from jax.experimental.pallas import tpu as pltpu
from jax.sharding import PartitionSpec as P

BOTH = ("rows", "rep")
VMEM = pl.BlockSpec(memory_space=pltpu.VMEM)
SMEM = pl.BlockSpec(memory_space=pltpu.SMEM)


def digit_groups(owners):
    top = owners.bit_length() - 1
    groups = []
    while top > 0:
        take = min(2, top)
        top -= take
        groups.append((top, 1 << take))
    return groups


def across(value, mask, owners, swap):
    pairs = [(i, i ^ (2 * mask + swap)) for i in range(2 * owners)]
    return lax.ppermute(value, BOTH, pairs)


def half_kernel(features, keep, sem):
    half, _ = keep.shape
    side = lax.axis_index("rep")
    copy = pltpu.make_async_copy(features.at[pl.ds(pl.multiple_of(side * half, half), half), :], keep, sem)
    copy.start()
    copy.wait()


def own_half(features):
    return pl.pallas_call(
        half_kernel,
        out_shape=jax.ShapeDtypeStruct((features.shape[0] // 2, features.shape[1]), features.dtype),
        in_specs=[pl.BlockSpec(memory_space=pltpu.HBM)],
        out_specs=VMEM,
        scratch_shapes=[pltpu.SemaphoreType.DMA],
        compiler_params=pltpu.CompilerParams(vmem_limit_bytes=8 << 20),
        name="own_half",
    )(pltpu.with_memory_space_constraint(features, pltpu.HBM))


def copy_kernel(value, out):
    out[...] = value[...]


def copies(value, count):
    out = [value]
    while len(out) < count:
        one = pl.pallas_call(
            copy_kernel,
            out_shape=jax.ShapeDtypeStruct(value.shape, value.dtype),
            in_specs=[VMEM],
            out_specs=VMEM,
            compiler_params=pltpu.CompilerParams(vmem_limit_bytes=16 << 20),
            name="copy",
        )(out[-1])
        out.append(one)
    return out


def limit(owners):
    return pltpu.CompilerParams(vmem_limit_bytes=(8 if owners <= 16 else 48) << 20)


def place_kernel(groups, counts, cols, vals, weight, bias, dense, weight_out, bias_out):
    nblk, slots, flat = vals.shape
    owners = dense.shape[0]
    weight_out[...] = weight[...].astype(jnp.float32).T.astype(jnp.bfloat16)
    bias_out[...] = jnp.broadcast_to(bias[...], (128, bias.shape[1])).T
    wide = flat // 128
    deep = 16 * slots
    lane = lax.broadcasted_iota(jnp.int32, (slots, deep), 1)
    slot = lax.broadcasted_iota(jnp.int32, (slots, deep), 0)
    spread = (lane % slots == slot).astype(jnp.bfloat16)
    named = jnp.dot(cols[...].astype(jnp.bfloat16), spread, preferred_element_type=jnp.float32)
    named = named.astype(jnp.int32)
    apart = (named >> 1) ^ lax.axis_index("rows")
    place = jnp.zeros_like(apart)
    stride = 1
    for shift, radix in groups:
        place = place + ((apart >> shift) & (radix - 1)) * stride
        stride *= radix
    side = named & 1
    lane = lax.broadcasted_iota(jnp.int32, (1, deep), 1)
    at = lax.broadcasted_iota(jnp.int32, (256, deep), 0)
    same = at % 16 == lax.broadcasted_iota(jnp.int32, (256, deep), 1) // slots
    low = lax.broadcasted_iota(jnp.int32, (slots, 128), 1) < 64
    for r in range(nblk):
        used = lane % slots < counts[0, r]
        to_first = jnp.where(used & (side[r : r + 1] == 0), place[r : r + 1], -1)
        to_second = jnp.where(used & (side[r : r + 1] == 1), place[r : r + 1], -1)
        rights = []
        for g in range(wide // 16):
            top, bottom = [], []
            for i in range(g * 16, g * 16 + 16):
                two = vals[r, :, i * 128 : (i + 1) * 128].astype(jnp.float32)
                turned = pltpu.roll(two, 64, 1)
                both = jnp.concatenate([jnp.where(low, two, 0.0), jnp.where(low, turned, 0.0)], axis=1)
                top.append(both.astype(jnp.bfloat16))
                both = jnp.concatenate([jnp.where(low, 0.0, turned), jnp.where(low, 0.0, two)], axis=1)
                bottom.append(both.astype(jnp.bfloat16))
            rights.append(jnp.concatenate(top + bottom, axis=0))

        def put(q):
            here = at // 16 + q * 16
            pick = jnp.concatenate([same & (here == to_first), same & (here == to_second)], axis=1)
            pick = pick.astype(jnp.bfloat16)
            for g, right in enumerate(rights):
                moved = jnp.dot(pick, right, preferred_element_type=jnp.float32).astype(jnp.bfloat16)
                moved = moved.reshape(16, 16, 256)
                start = r * wide + g * 16
                dense[pl.ds(q * 16, 16), start : start + 16, :] = moved[:, :, :128]
                start += nblk * wide
                dense[pl.ds(q * 16, 16), start : start + 16, :] = moved[:, :, 128:]

        if owners <= 16:
            put(0)
        else:
            pl.loop(0, owners // 16)(put)


def place_blocks(counts, cols, vals, weight, bias, owners):
    nblk, slots, flat = vals.shape
    wide = flat // 128
    return pl.pallas_call(
        functools.partial(place_kernel, digit_groups(owners)),
        out_shape=(
            jax.ShapeDtypeStruct((owners, 2 * nblk * wide, 128), jnp.bfloat16),
            jax.ShapeDtypeStruct(weight.shape[::-1], weight.dtype),
            jax.ShapeDtypeStruct((bias.shape[1], 128), bias.dtype),
        ),
        in_specs=[SMEM] + [VMEM] * 4,
        out_specs=(VMEM,) * 3,
        compiler_params=limit(owners),
        name="place",
    )(counts, cols, vals, weight, bias)


def sum_kernel(places, last, dense, *refs):
    pieces, out = refs[:-1], refs[-1]
    rows = dense.shape[1]
    if last:
        acc, pieces = pieces[0][...], pieces[1:]
    else:
        acc = jnp.zeros((rows, 128), jnp.float32)
    for start, feats in zip(places, pieces):
        each = feats.shape[0] // 128

        def two(q, acc):
            left = jnp.concatenate([dense[start + 2 * q], dense[start + 2 * q + 1]], axis=1)
            right = feats[pl.ds(pl.multiple_of(q * 256, 256), 256), :]
            return acc + jnp.dot(left, right, preferred_element_type=jnp.float32)

        if each <= 16:
            for q in range(each // 2):
                acc = two(q, acc)
        else:
            acc = lax.fori_loop(0, each // 2, two, acc)
    out[...] = acc


def sum_blocks(dense, operands, places, last):
    return pl.pallas_call(
        functools.partial(sum_kernel, places, last),
        out_shape=jax.ShapeDtypeStruct((dense.shape[1], 128), jnp.float32),
        in_specs=[VMEM] * (1 + len(operands)),
        out_specs=VMEM,
        compiler_params=limit(dense.shape[0]),
        name="block_sum",
    )(dense, *operands)


def node_at(place, nodes):
    rest = place % (nodes // 2)
    return rest // 32 * 64 + rest % 32 * 2 + place // (nodes // 2)


def turn_kernel(mine, other, turned):
    first = lax.axis_index("rep") == 0
    here, there = mine[...].astype(jnp.float32), other[...].astype(jnp.float32)
    both = jnp.concatenate([jnp.where(first, here, there), jnp.where(first, there, here)], axis=0)
    nodes = both.shape[0]
    wanted = node_at(lax.broadcasted_iota(jnp.int32, (nodes, nodes), 0), nodes)
    order = (wanted == lax.broadcasted_iota(jnp.int32, (nodes, nodes), 1)).astype(jnp.bfloat16)
    both = jnp.dot(order, both.astype(jnp.bfloat16), preferred_element_type=jnp.float32)
    turned[...] = both.T.astype(turned.dtype)


def turn(mine, other):
    half, wide = mine.shape
    return pl.pallas_call(
        turn_kernel,
        out_shape=jax.ShapeDtypeStruct((wide, 2 * half), mine.dtype),
        in_specs=[VMEM, VMEM],
        out_specs=VMEM,
        compiler_params=limit(16),
        name="turn",
    )(mine, other)


NT = (((1,), (1,)), ((), ()))


def layer_kernel(mine, other, weight, bias, weight_t, bias_t, cot_t, parts, act):
    owners, chunk, _ = parts.shape
    share = weight_t.shape[0] // owners
    aggregated = (mine[...] + other[...]).astype(jnp.bfloat16)
    pre = lax.dot_general(weight_t[...], aggregated, NT, preferred_element_type=jnp.float32)
    pre = pre + jnp.concatenate([bias_t[...]] * (pre.shape[1] // 128), axis=1)
    sig = 1.0 / (1.0 + jnp.exp(-pre))
    cot = cot_t[...].astype(jnp.float32)
    delta = (cot * sig * (1.0 + pre * (1.0 - sig))).astype(jnp.bfloat16)
    half = act.shape[0]
    own = lax.broadcasted_iota(jnp.int32, (half, 2 * half), 0) + lax.axis_index("rep") * half
    found = node_at(lax.broadcasted_iota(jnp.int32, (half, 2 * half), 1), 2 * half)
    nodes = jnp.dot((found == own).astype(jnp.bfloat16), aggregated, preferred_element_type=jnp.float32)
    value = jnp.dot(nodes.astype(jnp.bfloat16), weight[...], preferred_element_type=jnp.float32) + bias[...]
    act[...] = (value / (1.0 + jnp.exp(-value))).astype(act.dtype)
    grad = jnp.dot(delta, aggregated, preferred_element_type=jnp.float32)
    ones = jnp.ones((16, delta.shape[1]), jnp.bfloat16)
    total = lax.dot_general(ones, delta, NT, preferred_element_type=jnp.float32)[:1]
    blank = jnp.zeros((chunk - share - 2, 128), jnp.float32)
    tail = jnp.concatenate([total[:, :128], total[:, 128:], blank], axis=0)
    for r in range(owners):
        parts[r] = jnp.concatenate([grad[r * share : (r + 1) * share], tail], axis=0).astype(parts.dtype)


def layer(mine, other, weight, bias, weight_t, bias_t, cot_t, owners):
    share = weight_t.shape[0] // owners
    chunk = -(-(share + 2) // 16) * 16
    return pl.pallas_call(
        layer_kernel,
        out_shape=(
            jax.ShapeDtypeStruct((owners, chunk, 128), jnp.bfloat16),
            jax.ShapeDtypeStruct((mine.shape[0] // 2, weight.shape[1]), jnp.bfloat16),
        ),
        in_specs=[VMEM] * 7,
        out_specs=(VMEM, VMEM),
        compiler_params=limit(owners),
        name="layer",
    )(mine, other, weight, bias, weight_t, bias_t, cot_t)


def finish_kernel(act_in, got, act, weight_grad, bias_grad):
    act[...] = act_in[...]
    share = weight_grad.shape[0]
    total = jnp.sum(got[...].astype(jnp.float32), axis=0)
    weight_grad[...] = total[:share]
    flat = jnp.concatenate([total[share : share + 1], total[share + 1 : share + 2]], axis=1)
    flat = jnp.broadcast_to(flat, (8, 256))
    flat = pltpu.roll(flat, lax.rem(256 - lax.axis_index("rows") * share, 256), 1)
    bias_grad[...] = flat[:1, :share]


def finish(act, got):
    owners = got.shape[0]
    share = act.shape[1] // owners
    return pl.pallas_call(
        finish_kernel,
        out_shape=(
            jax.ShapeDtypeStruct(act.shape, act.dtype),
            jax.ShapeDtypeStruct((share, 128), jnp.float32),
            jax.ShapeDtypeStruct((1, share), jnp.float32),
        ),
        in_specs=[VMEM] * 2,
        out_specs=(VMEM,) * 3,
        compiler_params=limit(owners),
        name="finish",
    )(act, got)


def body(features, weight, bias, block_count, block_cols, block_vals, cotangent):
    owners = lax.axis_size("rows")
    groups = digit_groups(owners)

    keep = own_half(features)
    shift, radix = groups[0]
    sent = zip(range(1, radix), copies(keep, radix - 1))
    pieces = [keep] + [across(value, s << shift, owners, 0) for s, value in sent]
    vals = block_vals[0]
    for shift, radix in groups[1:]:
        held, vals, cotangent = lax.optimization_barrier((jnp.concatenate(pieces), vals, cotangent))
        sent = zip(range(1, radix), copies(held, radix - 1))
        pieces = [held] + [across(value, s << shift, owners, 0) for s, value in sent]

    bias = bias.reshape(1, -1)
    dense, weight_t, bias_t = place_blocks(block_count, block_cols[0], vals, weight, bias, owners)
    cot_t = turn(cotangent, across(cotangent, 0, owners, 1))
    dense, cot_t = lax.optimization_barrier((dense, cot_t))
    each = pieces[0].shape[0] // 128
    places = [s * each for s in range(len(pieces))]
    ends = (0, len(pieces) - 1)
    early = sum_blocks(dense, [pieces[s] for s in ends], [places[s] for s in ends], False)
    late = [s for s in range(len(pieces)) if s not in ends]
    mine = sum_blocks(dense, [early] + [pieces[s] for s in late], [places[s] for s in late], True)
    other = across(mine, 0, owners, 1)
    parts, activated = layer(mine, other, weight, bias, weight_t, bias_t, cot_t, owners)
    got = lax.all_to_all(parts, "rows", split_axis=0, concat_axis=0, tiled=True)
    activated, weight_grad, bias_grad = finish(activated, got)
    return activated, weight_grad.T, bias_grad.reshape(-1)


def solution(mesh):
    placed = (
        P("rows", None),
        P(),
        P(),
        P("rep", "rows"),
        P("rep", "rows", None),
        P("rep", "rows", None, None),
        P(BOTH, None),
    )
    return jax.shard_map(
        body,
        mesh=mesh,
        in_specs=placed,
        out_specs=(P(BOTH, None), P(None, "rows"), P("rows")),
        check_vma=False,
    )
```
